256 devices in a mesh: gx: 8 (over x, core), gy: 32 (over z, y).
Axes of the slice: x: 4, y: 4, z: 8, core: 2. Of those that a mesh axis runs over, the one named last changes fastest.
Arguments:
- start: float32 [256, 1024, 128], P('gx', 'gy')
- velocity: float32 [3, 256, 1024, 128], P(None, 'gx', 'gy'), may hold values from -1 to 1
- prior: float32 [8, 256, 1024, 128], P(None, 'gx', 'gy')
- shifts: float32 [8], replicated, may hold values from 0.05 to 1.95, as said below
Outputs:
- basis_new: float32 [9, 256, 1024, 128], P(None, 'gx', 'gy')
- coeffs: float32 [17, 9], replicated
The draws below stay inside these ranges and needn't reach their ends.
Inputs may be any that keep to these rules, and one draw needn't show every extreme that they name: Newton shifts, one in each of 8 spread places over the operator's real range, in an order drawn from the seed.
All inputs are finite; a program needn't handle non-finite values.
Results may differ from the reference program's by a relative error of at most 0.0003.
Values sent between devices are 32-bit elements; how exact they have to be, the bound alone decides.
No kernel may reach another device: no remote copies, remote signals or barrier semaphores. Data moves between devices by JAX's collectives and lax.ppermute only.
A program may use at most 64 MiB of HBM per device.

```python
import math
import jax
import jax.numpy as jnp
from jax import lax

STEPS = 8
PRIOR = 8
NX = 256
NY = 1024
NZ = 128


def shared_fields(key):
    normal = jax.random.normal(key, (PRIOR, NX, NY, NZ), jnp.float32)
    scale_key = jax.random.fold_in(key, 7)
    factors = jnp.exp(jax.random.uniform(scale_key, (PRIOR,), jnp.float32, -0.7, 0.7))
    return factors[:, None, None, None] * normal


def draw_prior(key, part):
    fields = shared_fields(key)
    return fields


def draw_start(key, part):
    fields = shared_fields(key)
    span = math.log(10.0)
    key = jax.random.fold_in(key, 3)
    key_mix, key_sign, key_amp, key_noise, key_plane = jax.random.split(key, 5)
    weights = jax.random.uniform(key_mix, (PRIOR,), jnp.float32, 0.3, 1.0)
    signs = jnp.where(jax.random.bernoulli(key_sign, 0.5, (PRIOR,)), 1.0, -1.0).astype(jnp.float32)
    weights = weights * signs
    levels = jax.random.uniform(key_amp, (NX, NY, 1), jnp.float32, 0.0, 1.0)
    plane_levels = jax.random.uniform(key_plane, (1, 1, NZ), jnp.float32, 0.0, 1.0)
    amplitude = 0.4 * jnp.exp(span * levels) * jnp.exp(math.log(4.0) * plane_levels)
    noise = jax.random.normal(key_noise, (NX, NY, NZ), jnp.float32)
    mixed = jnp.sum(weights[:, None, None, None] * fields, axis=0)
    return 0.6 * mixed + amplitude * noise


def draw_shifts(key, part):
    key = jax.random.fold_in(key, 5)
    key_order, key_jitter = jax.random.split(key)
    order = jax.random.permutation(key_order, STEPS).astype(jnp.float32)
    jitter = jax.random.uniform(key_jitter, (STEPS,), jnp.float32, -0.05, 0.05)
    return 1.0 + 0.82 * jnp.cos(math.pi * (order + 0.5) / STEPS) + jitter


def block_scale(key, shape, shards, least, high):
    def one(position, shards_of):
        steps = jax.random.uniform(jax.random.fold_in(jax.random.fold_in(key, 6), position), (shards_of,), jnp.float32, least / len(shards), high / len(shards))
        return jnp.repeat(jnp.exp(steps), shape[position] // shards_of).reshape((-1,) + (1,) * (len(shape) - position - 1))

    loudness = one(*shards[0])
    for cut in shards[1:]:
        loudness = loudness * one(*cut)
    return loudness


def setup_inputs(seed: int = 0) -> dict:
    key_of = jax.random.split(jax.random.key(seed), 5)
    return {
        "start": draw_start(jax.random.fold_in(key_of[4], 71), 0),
        "velocity": jnp.clip(jax.random.uniform(key_of[1], (3, NX, NY, NZ), jnp.float32, -1.0, 1.0) * block_scale(key_of[1], (3, NX, NY, NZ), ((1, 8), (2, 32)), -0.4, 0.0), -1.0, 1.0),
        "prior": draw_prior(jax.random.fold_in(key_of[4], 71), 0),
        "shifts": draw_shifts(jax.random.fold_in(key_of[4], 71), 0),
    }


drift_scale = 0.3

def apply_step(padded, flow, shift):
    center = padded[1:-1, 1:-1]
    east = padded[2:, 1:-1]
    west = padded[:-2, 1:-1]
    north = padded[1:-1, 2:]
    south = padded[1:-1, :-2]
    plane = jnp.zeros_like(center[:, :, :1])
    upper = jnp.concatenate([center[:, :, 1:], plane], axis=2)
    below = jnp.concatenate([plane, center[:, :, :-1]], axis=2)
    neighbours = east + west + north + south + upper + below
    drift = flow[0] * (east - west) + flow[1] * (north - south) + flow[2] * (upper - below)
    return center - neighbours / 6.0 + drift_scale * drift - shift * center

def reference(start, velocity, prior, shifts):
    vectors = [start]
    field = start
    for step in range(STEPS):
        field = apply_step(jnp.pad(field, ((1, 1), (1, 1), (0, 0))), velocity, shifts[step])
        vectors.append(field)
    basis = jnp.stack(vectors).reshape(STEPS + 1, -1)
    prior_rows = prior.reshape(PRIOR, -1)
    count = float(NX * NY * NZ)
    proj_coeff = jnp.dot(prior_rows, basis.T, precision=lax.Precision.HIGHEST) / count
    projected = basis - jnp.dot(proj_coeff.T, prior_rows, precision=lax.Precision.HIGHEST)
    gram = jnp.dot(projected, projected.T, precision=lax.Precision.HIGHEST) / count
    lower = jnp.linalg.cholesky(gram)
    identity = jnp.eye(STEPS + 1, dtype=gram.dtype)
    inverse = jax.scipy.linalg.solve_triangular(lower, identity, lower=True)
    basis_new = jnp.dot(inverse, projected, precision=lax.Precision.HIGHEST).reshape(STEPS + 1, NX, NY, NZ)
    coeffs = jnp.concatenate([proj_coeff, lower.T], axis=0)
    return (basis_new, coeffs)
```

```python
import functools

import jax
import jax.numpy as jnp
import numpy as np
from jax import lax
from jax.experimental import pallas as pl
from jax.experimental.pallas import tpu as pltpu
from jax.sharding import PartitionSpec as P

STEPS = 8
PRIOR = 8
NEW = STEPS + 1
FIELDS = PRIOR + NEW
H = STEPS
DRIFT = 0.3
AXES = ("gx", "gy")

EARLY = [(i, j) for i in range(9) for j in range(i, 9)]
LATE = [(i, j) for i in range(9, 17) for j in range(i, 17)]
CROSS = [[(i, j) for i in range(9) for j in range(lo, lo + 4)] for lo in (9, 13)]
PAIRS = EARLY + LATE + CROSS[0] + CROSS[1]
SLOTS = 160


def pair_tables():
    first = np.zeros((128, 256), np.float32)
    second = np.zeros((128, 256), np.float32)
    for p, (i, j) in enumerate(PAIRS):
        first[i, p] = 0.5 if i == j else 1.0
        second[j, p] = 1.0
    return first, second


def products(load, pairs, groups):
    used = sorted({f for pair in pairs for f in pair})

    def body(g, totals):
        tile = {f: load(f, g) for f in used}
        return tuple(t + tile[i] * tile[j] for t, (i, j) in zip(totals, pairs))

    zero = jnp.zeros((8, 128), jnp.float32)
    return lax.fori_loop(0, groups, body, (zero,) * len(pairs), unroll=2)


def tile_of(ref, field, g, blocks):
    x, y = g // blocks, g % blocks
    rows = pl.ds(pl.multiple_of(y * 8, 8), 8)
    return ref[x, rows, :] if field is None else ref[field, x, rows, :]


def early_kernel(prior_ref, start_ref, out_ref):
    blocks = start_ref.shape[1] // 8
    groups = start_ref.shape[0] * blocks

    def load(f, g):
        return tile_of(prior_ref, f, g, blocks) if f < 8 else tile_of(start_ref, None, g, blocks)

    for p, total in enumerate(products(load, EARLY, groups)):
        out_ref[p] = total


def stencil_kernel(
    shifts_ref, sides_ref, start_ref, vel_ref, yl_ref, yh_ref, xl_ref, xh_ref, cl_ref, ch_ref, prior_ref, early_ref,
    basis_ref, sums_ref,
    fld, alt, down, pri, sta, acc, sems,
):
    wx, wy = sta.shape[0], sta.shape[1]
    ex, ey = wx + 2 * H, wy + 2 * H
    o = 2 * H
    mid_x, mid_y = pl.ds(H, wx), pl.ds(o, wy)
    low_y, high_y = pl.ds(H, H), pl.ds(o + wy, H)
    low_x, high_x = pl.ds(0, H), pl.ds(H + wx, H)
    copies = [
        (start_ref, fld.at[0, mid_x, mid_y]),
        (vel_ref, fld.at[pl.ds(1, 3), mid_x, mid_y]),
        (yl_ref, fld.at[:, mid_x, low_y]),
        (yh_ref, fld.at[:, mid_x, high_y]),
        (xl_ref, fld.at[:, low_x, mid_y]),
        (xh_ref, fld.at[:, high_x, mid_y]),
        (cl_ref.at[:, :, pl.ds(0, H)], fld.at[:, low_x, low_y]),
        (cl_ref.at[:, :, pl.ds(H, H)], fld.at[:, low_x, high_y]),
        (ch_ref.at[:, :, pl.ds(0, H)], fld.at[:, high_x, low_y]),
        (ch_ref.at[:, :, pl.ds(H, H)], fld.at[:, high_x, high_y]),
        (start_ref, sta),
        (prior_ref, pri),
    ]
    copies = [pltpu.make_async_copy(src, dst, sems.at[k]) for k, (src, dst) in enumerate(copies)]
    for c in copies:
        c.start()
    for c in copies[:10]:
        c.wait()

    x_low, x_high, y_low, y_high = (sides_ref[k] for k in range(4))
    lane = lax.broadcasted_iota(jnp.int32, (1, 1, 128), 2)
    not_last = jnp.where(lane < 127, 1.0, 0.0)
    not_first = jnp.where(lane > 0, 1.0, 0.0)
    sixth = 1.0 / 6.0

    def rows_of(step, x, n, x_side):
        src, dst = (fld.at[0], alt) if step % 2 == 0 else (alt, fld.at[0])
        last = step == STEPS - 1
        lo, size = (o, wy) if last else (H, ey)
        keep = 1.0 - shifts_ref[step]
        here, ys = pl.ds(x, n), pl.ds(lo, size)
        c = src[here, ys, :]
        e, w = src[pl.ds(x + 1, n), ys, :], src[pl.ds(x - 1, n), ys, :]
        u, d = src[here, pl.ds(lo + 1, size), :], src[here, pl.ds(lo - 1, size), :]
        if step == 0:
            a0, a1 = DRIFT * fld[1, here, ys, :], DRIFT * fld[2, here, ys, :]
            a2 = DRIFT * fld[3, here, ys, :]
            up, dn = (a2 - sixth) * not_last, (-a2 - sixth) * not_first
            fld[1, here, ys, :], fld[2, here, ys, :] = a0, a1
            fld[3, here, ys, :], down[here, ys, :] = up, dn
        else:
            a0, a1 = fld[1, here, ys, :], fld[2, here, ys, :]
            up, dn = fld[3, here, ys, :], down[here, ys, :]
        above = pltpu.roll(c, 127, 2)
        below = pltpu.roll(c, 1, 2)
        r = keep * c - sixth * ((e + w) + (u + d)) + a0 * (e - w) + a1 * (u - d) + (up * above + dn * below)
        if x_side is None:
            basis_ref[step, pl.ds(x - H, n), :, :] = r if last else r[:, H : H + wy]
        if last:
            return
        ml, mh = y_low, y_high
        middle = r[:, H : H + wy]
        if x_side is not None:
            ml, mh, middle = ml * x_side, mh * x_side, middle * x_side
        dst[here, low_y, :] = r[:, :H] * ml
        dst[here, mid_y, :] = middle
        dst[here, high_y, :] = r[:, H + wy :] * mh

    for step in range(STEPS):
        side = STEPS - 1 - step
        for k in range(side):
            rows_of(step, H - 1 - k, 1, x_low)
            rows_of(step, H + wx + k, 1, x_high)

        def some(i, carry, step=step):
            rows_of(step, H + i * 2, 2, None)
            return carry

        lax.fori_loop(0, wx // 2, some, 0)

    for c in copies[10:]:
        c.wait()
    blocks = wy // 8
    groups = wx * blocks

    def load(f, g):
        if f < 8:
            return tile_of(pri, f, g, blocks)
        return tile_of(sta, None, g, blocks) if f == 8 else tile_of(basis_ref, f - 9, g, blocks)

    n = len(EARLY)
    acc[0 : n * 8, :] = early_ref[...].reshape(n * 8, 128)
    for pairs in (LATE, *CROSS):
        for p, total in enumerate(products(load, pairs, groups)):
            acc[(n + p) * 8 : (n + p) * 8 + 8, :] = total
        n += len(pairs)
    acc[n * 8 :, :] = jnp.zeros((SLOTS * 8 - n * 8, 128), jnp.float32)
    by_lane = acc[pl.ds(0, SLOTS, stride=8), :]
    for s in range(1, 8):
        by_lane = by_lane + acc[pl.ds(s, SLOTS, stride=8), :]
    total = lax.dot_general(
        jnp.ones((8, 128), jnp.float32), by_lane, (((1,), (1,)), ((), ())),
        precision=lax.Precision.HIGHEST, preferred_element_type=jnp.float32,
    )
    second = jnp.concatenate([total[:, 128:], jnp.zeros((8, 256 - SLOTS), jnp.float32)], axis=1)
    even = lax.broadcasted_iota(jnp.int32, (8, 128), 0) % 2 == 0
    both = jnp.where(even, total[:, :128], second)
    for k in range(sums_ref.shape[0] // 8):
        sums_ref[k * 8 : k * 8 + 8, :] = both


def combine_kernel(
    count, chunks,
    sums_ref, first_ref, second_ref, start_hbm, basis_hbm, prior_hbm,
    new_hbm, coeffs_ref,
    bas, pri, new, spread, in_sems, out_sems,
):
    wx, wy = bas.shape[1], bas.shape[2]
    part = wx // chunks
    loads = []
    for k in range(chunks):
        xs = pl.ds(k * part, part)
        loads.append([
            pltpu.make_async_copy(start_hbm.at[xs], bas.at[0, xs], in_sems.at[k, 0]),
            pltpu.make_async_copy(basis_hbm.at[:, xs], bas.at[pl.ds(1, STEPS), xs], in_sems.at[k, 1]),
            pltpu.make_async_copy(prior_hbm.at[:, xs], pri.at[:, xs], in_sems.at[k, 2]),
        ])
    for group in loads:
        for c in group:
            c.start()

    total = sums_ref[0:8, :]
    for k in range(1, sums_ref.shape[0] // 8):
        total = total + sums_ref[k * 8 : k * 8 + 8, :]
    total = total + pltpu.roll(total, 4, 0)
    total = (total + pltpu.roll(total, 2, 0)) * (1.0 / count)
    flat = jnp.concatenate([total[0:1, :], total[1:2, :]], axis=1)
    contract = functools.partial(
        lax.dot_general, dimension_numbers=(((1,), (1,)), ((), ())),
        precision=lax.Precision.HIGHEST, preferred_element_type=jnp.float32,
    )
    first, second = first_ref[...], second_ref[...]
    full = contract(first[:24] * flat, second) + contract(second[:24] * flat, first)
    top, low = full[0:8, :], full[8:24, :]
    inner = 2.0 * top
    for k in range(PRIOR):
        inner = inner - top[:, k : k + 1] * top[k : k + 1, :]
    gram = low
    for k in range(PRIOR):
        gram = gram - low[:, k : k + 1] * inner[k : k + 1, :]
    lane = lax.broadcasted_iota(jnp.int32, (16, 128), 1)
    row = lax.broadcasted_iota(jnp.int32, (16, 128), 0)
    work = jnp.where(lane < NEW, pltpu.roll(gram, 128 - PRIOR, 1), 0.0)
    work = work + jnp.where(lane == row + 16, 1.0, 0.0)
    work = work + jnp.where((lane >= 32) & (lane < 32 + PRIOR), pltpu.roll(low, 32, 1), 0.0)
    for k in range(NEW):
        pivot = work[k : k + 1, k : k + 1]
        scaled = work[k : k + 1, :] / jnp.sqrt(pivot)
        column = work[:, k : k + 1] / pivot
        work = jnp.where(row > k, work - column * work[k : k + 1, :], jnp.where(row == k, scaled, work))
    coeffs_ref[0:PRIOR, :] = pltpu.roll(top, 128 - PRIOR, 1)[:, :NEW]
    coeffs_ref[PRIOR:FIELDS, :] = jnp.where(lane >= row, work, 0.0)[:NEW, :NEW]
    for i in range(FIELDS):
        at = 16 + i if i < NEW else 32 + i - NEW
        spread[i] = jnp.broadcast_to(work[:, at : at + 1], (16, 128))

    stores = []
    for k in range(chunks):
        for c in loads[k]:
            c.wait()

        def some(g, carry, k=k):
            x, y = k * part + g // (wy // 16), g % (wy // 16)
            ys = pl.ds(pl.multiple_of(y * 16, 16), 16)
            tiles = [bas[i, x, ys, :] for i in range(NEW)] + [pri[i, x, ys, :] for i in range(PRIOR)]
            for j in range(NEW):
                r = spread[0, j : j + 1, :] * tiles[0]
                for i in range(1, j + 1):
                    r = r + spread[i, j : j + 1, :] * tiles[i]
                for i in range(NEW, FIELDS):
                    r = r - spread[i, j : j + 1, :] * tiles[i]
                new[j, x, ys, :] = r
            return carry

        lax.fori_loop(0, part * (wy // 16), some, 0)
        xs = pl.ds(k * part, part)
        stores.append(pltpu.make_async_copy(new.at[:, xs], new_hbm.at[:, xs], out_sems.at[k]))
        stores[-1].start()
    for c in stores:
        c.wait()


def on_device(start, velocity, prior, shifts):
    wx, wy, wz = start.shape
    nx, ny = lax.axis_size("gx"), lax.axis_size("gy")
    devices = nx * ny
    ahead_x, ahead_y = ([(i, i + 1) for i in range(n - 1)] for n in (nx, ny))
    back_x, back_y = ([(i + 1, i) for i in range(n - 1)] for n in (nx, ny))

    def edge(at, dim):
        cut = [slice(None)] * 3
        cut[dim] = slice(at, at + H)
        return jnp.concatenate([start[tuple(cut)][None], velocity[(slice(None), *cut)]], axis=0)

    yl = lax.ppermute(edge(wy - H, 1), "gy", ahead_y)
    yh = lax.ppermute(edge(0, 1), "gy", back_y)
    xl = lax.ppermute(edge(wx - H, 0), "gx", ahead_x)
    xh = lax.ppermute(edge(0, 0), "gx", back_x)
    cl = lax.ppermute(jnp.concatenate([yl[:, wx - H :], yh[:, wx - H :]], axis=2), "gx", ahead_x)
    ch = lax.ppermute(jnp.concatenate([yl[:, :H], yh[:, :H]], axis=2), "gx", back_x)
    ix, iy = lax.axis_index("gx"), lax.axis_index("gy")
    sides = jnp.stack([ix > 0, ix < nx - 1, iy > 0, iy < ny - 1]).astype(jnp.float32)

    f32 = jnp.float32
    vmem = pl.BlockSpec(memory_space=pltpu.VMEM)
    smem = pl.BlockSpec(memory_space=pltpu.SMEM)
    hbm = pl.BlockSpec(memory_space=pl.ANY)
    limit = pltpu.CompilerParams(vmem_limit_bytes=48 * 1024 * 1024)
    early = pl.pallas_call(
        early_kernel,
        out_shape=jax.ShapeDtypeStruct((len(EARLY), 8, 128), f32),
        in_specs=[vmem, vmem],
        out_specs=vmem,
        compiler_params=limit,
        name="early",
    )(prior, start)
    ex, ey = wx + 2 * H, wy + 4 * H
    basis, sums = pl.pallas_call(
        stencil_kernel,
        out_shape=(
            jax.ShapeDtypeStruct((STEPS, wx, wy, wz), f32),
            jax.ShapeDtypeStruct((devices * 2, 128), f32),
        ),
        in_specs=[smem, smem] + [hbm] * 9 + [vmem],
        out_specs=(vmem, vmem),
        scratch_shapes=[
            pltpu.VMEM((4, ex, ey, wz), f32),
            pltpu.VMEM((ex, ey, wz), f32),
            pltpu.VMEM((ex, ey, wz), f32),
            pltpu.VMEM((PRIOR, wx, wy, wz), f32),
            pltpu.VMEM((wx, wy, wz), f32),
            pltpu.VMEM((SLOTS * 8, 128), f32),
            pltpu.SemaphoreType.DMA((12,)),
        ],
        compiler_params=limit,
        name="stencil",
    )(shifts, sides, start, velocity, yl, yh, xl, xh, cl, ch, prior, early)
    every = lax.all_to_all(sums, AXES, 0, 0, tiled=True)
    chunks = 4
    first, second = pair_tables()
    basis_new, coeffs = pl.pallas_call(
        functools.partial(combine_kernel, float(devices * wx * wy * wz), chunks),
        out_shape=(
            jax.ShapeDtypeStruct((NEW, wx, wy, wz), f32),
            jax.ShapeDtypeStruct((FIELDS, NEW), f32),
        ),
        in_specs=[vmem, vmem, vmem, hbm, hbm, hbm],
        out_specs=(hbm, vmem),
        scratch_shapes=[
            pltpu.VMEM((NEW, wx, wy, wz), f32),
            pltpu.VMEM((PRIOR, wx, wy, wz), f32),
            pltpu.VMEM((NEW, wx, wy, wz), f32),
            pltpu.VMEM((FIELDS, 16, 128), f32),
            pltpu.SemaphoreType.DMA((chunks, 3)),
            pltpu.SemaphoreType.DMA((chunks,)),
        ],
        compiler_params=limit,
        name="combine",
    )(every, jnp.asarray(first), jnp.asarray(second), start, basis, prior)
    return basis_new, coeffs


def solution(mesh):
    return jax.shard_map(
        on_device,
        mesh=mesh,
        in_specs=(P("gx", "gy", None), P(None, "gx", "gy", None), P(None, "gx", "gy", None), P()),
        out_specs=(P(None, "gx", "gy", None), P()),
        check_vma=False,
    )
```

```python
import functools

import jax
import jax.numpy as jnp
import numpy as np
from jax import lax
from jax.experimental import pallas as pl
from jax.experimental.pallas import tpu as pltpu
from jax.sharding import PartitionSpec as P

STEPS = 8
PRIOR = 8
NEW = STEPS + 1
FIELDS = PRIOR + NEW
H = STEPS
DRIFT = 0.3
AXES = ("gx", "gy")

EARLY = [(i, j) for i in range(9) for j in range(i, 9)]
LATE = [(i, j) for i in range(9, 17) for j in range(i, 17)]
CROSS = [[(i, j) for i in range(9) for j in range(lo, lo + 4)] for lo in (9, 13)]
PAIRS = EARLY + LATE + CROSS[0] + CROSS[1]
SLOTS = 160


def pair_tables():
    first = np.zeros((128, 256), np.float32)
    second = np.zeros((128, 256), np.float32)
    for p, (i, j) in enumerate(PAIRS):
        first[i, p] = 0.5 if i == j else 1.0
        second[j, p] = 1.0
    return first, second


def corner_rows():
    at, pieces = 0, []
    for d in range(1, H):
        for f in range(4):
            pieces.append((at, d, f, H - d))
            at += H - d
    return pieces


CORNER = 2 * sum(n for _, _, _, n in corner_rows())


def pack_kernel(start_ref, vel_ref, y_first, y_last, x_first, x_last, sems):
    wx, wy = start_ref.shape[0], start_ref.shape[1]
    full = slice(None)
    copies = []
    for out, cut in (
        (y_last, (full, pl.ds(wy - H, H))),
        (y_first, (full, pl.ds(0, H))),
        (x_last, (pl.ds(wx - H, H), full)),
        (x_first, (pl.ds(0, H), full)),
    ):
        copies.append((start_ref.at[cut], out.at[0]))
        copies.append((vel_ref.at[(full, *cut)], out.at[pl.ds(1, 3)]))
    copies = [pltpu.make_async_copy(src, dst, sems.at[k]) for k, (src, dst) in enumerate(copies)]
    for c in copies:
        c.start()
    for c in copies:
        c.wait()


def corner_kernel(xl_ref, xh_ref, up_ref, down_ref):
    wy = xl_ref.shape[2]
    for at, d, f, n in corner_rows():
        up_ref[at : at + n, :] = xl_ref[f, H - d, wy - n :, :]
        down_ref[at : at + n, :] = xl_ref[f, H - d, :n, :]
        at += CORNER // 2
        up_ref[at : at + n, :] = xh_ref[f, d - 1, wy - n :, :]
        down_ref[at : at + n, :] = xh_ref[f, d - 1, :n, :]


def products(load, pairs, groups, start=None):
    used = sorted({f for pair in pairs for f in pair})

    def body(g, totals):
        tile = {f: load(f, g) for f in used}
        return tuple(t + tile[i] * tile[j] for t, (i, j) in zip(totals, pairs))

    if start is None:
        start = (jnp.zeros((8, 128), jnp.float32),) * len(pairs)
    return lax.fori_loop(0, groups, body, start, unroll=8)


def tile_of(ref, field, g, blocks):
    x, y = g // blocks, g % blocks
    rows = pl.ds(pl.multiple_of(y * 8, 8), 8)
    return ref[x, rows, :] if field is None else ref[field, x, rows, :]


def early_kernel(prior_hbm, start_hbm, out_ref, prior_ref, start_ref, sems):
    wx, blocks = start_ref.shape[0], start_ref.shape[1] // 8
    parts = sems.shape[0]
    part = wx // parts
    copies = []
    for k in range(parts):
        xs = pl.ds(k * part, part)
        copies.append([
            pltpu.make_async_copy(prior_hbm.at[:, xs], prior_ref.at[:, xs], sems.at[k, 0]),
            pltpu.make_async_copy(start_hbm.at[xs], start_ref.at[xs], sems.at[k, 1]),
        ])
        for c in copies[-1]:
            c.start()

    totals = None
    for k in range(parts):
        for c in copies[k]:
            c.wait()

        def load(f, g, k=k):
            g = g + k * part * blocks
            return tile_of(prior_ref, f, g, blocks) if f < 8 else tile_of(start_ref, None, g, blocks)

        totals = products(load, EARLY, part * blocks, totals)
    for p, total in enumerate(totals):
        out_ref[p] = total


def stencil_kernel(
    shifts_ref, sides_ref, start_ref, vel_ref, yl_ref, yh_ref, xl_ref, xh_ref, cl_ref, ch_ref, prior_ref, early_ref,
    basis_ref, sums_ref,
    fld, alt, down, acc, sems,
):
    wx, wy = start_ref.shape[0], start_ref.shape[1]
    ex, ey = wx + 2 * H, wy + 2 * H
    o = 2 * H
    mid_x, mid_y = pl.ds(H, wx), pl.ds(o, wy)
    low_y, high_y = pl.ds(H, H), pl.ds(o + wy, H)
    low_x, high_x = pl.ds(0, H), pl.ds(H + wx, H)
    copies = [
        (start_ref, fld.at[0, mid_x, mid_y]),
        (vel_ref, fld.at[pl.ds(1, 3), mid_x, mid_y]),
        (yl_ref, fld.at[:, mid_x, low_y]),
        (yh_ref, fld.at[:, mid_x, high_y]),
        (xl_ref, fld.at[:, low_x, mid_y]),
        (xh_ref, fld.at[:, high_x, mid_y]),
    ]
    copies = [pltpu.make_async_copy(src, dst, sems.at[k]) for k, (src, dst) in enumerate(copies)]
    for c in copies:
        c.start()
    for at, d, f, n in corner_rows():
        fld[f, H - d, o - n : o, :] = cl_ref[at : at + n, :]
        fld[f, H - d, o + wy : o + wy + n, :] = ch_ref[at : at + n, :]
        at += CORNER // 2
        fld[f, H + wx - 1 + d, o - n : o, :] = cl_ref[at : at + n, :]
        fld[f, H + wx - 1 + d, o + wy : o + wy + n, :] = ch_ref[at : at + n, :]
    for c in copies:
        c.wait()

    x_low, x_high, y_low, y_high = (sides_ref[k] for k in range(4))
    lane = lax.broadcasted_iota(jnp.int32, (1, 1, 128), 2)
    not_last = jnp.where(lane < 127, 1.0, 0.0)
    not_first = jnp.where(lane > 0, 1.0, 0.0)
    sixth = 1.0 / 6.0

    def rows_of(step, x, n, x_side):
        src, dst = (fld.at[0], alt) if step % 2 == 0 else (alt, fld.at[0])
        last = step == STEPS - 1
        lo, size = (o, wy) if last else (H, ey)
        keep = 1.0 - shifts_ref[step]
        here, ys = pl.ds(x, n), pl.ds(lo, size)
        c = src[here, ys, :]
        e, w = src[pl.ds(x + 1, n), ys, :], src[pl.ds(x - 1, n), ys, :]
        u, d = src[here, pl.ds(lo + 1, size), :], src[here, pl.ds(lo - 1, size), :]
        if step == 0:
            a0, a1 = DRIFT * fld[1, here, ys, :], DRIFT * fld[2, here, ys, :]
            a2 = DRIFT * fld[3, here, ys, :]
            up, dn = (a2 - sixth) * not_last, (-a2 - sixth) * not_first
            fld[1, here, ys, :], fld[2, here, ys, :] = a0, a1
            fld[3, here, ys, :], down[here, ys, :] = up, dn
        else:
            a0, a1 = fld[1, here, ys, :], fld[2, here, ys, :]
            up, dn = fld[3, here, ys, :], down[here, ys, :]
        above = pltpu.roll(c, 127, 2)
        below = pltpu.roll(c, 1, 2)
        r = keep * c - sixth * ((e + w) + (u + d)) + a0 * (e - w) + a1 * (u - d) + (up * above + dn * below)
        if x_side is None:
            basis_ref[step, pl.ds(x - H, n), :, :] = r if last else r[:, H : H + wy]
        if last:
            return
        ml, mh = y_low, y_high
        middle = r[:, H : H + wy]
        if x_side is not None:
            ml, mh, middle = ml * x_side, mh * x_side, middle * x_side
        dst[here, low_y, :] = r[:, :H] * ml
        dst[here, mid_y, :] = middle
        dst[here, high_y, :] = r[:, H + wy :] * mh

    for step in range(STEPS):
        side = STEPS - 1 - step
        if side:
            rows_of(step, H - side, side, x_low)
            rows_of(step, H + wx, side, x_high)

        def some(i, carry, step=step):
            rows_of(step, H + i * 8, 8, None)
            return carry

        lax.fori_loop(0, wx // 8, some, 0)

    blocks = wy // 8
    groups = wx * blocks

    def load(f, g):
        if f < 8:
            return tile_of(prior_ref, f, g, blocks)
        return tile_of(start_ref, None, g, blocks) if f == 8 else tile_of(basis_ref, f - 9, g, blocks)

    n = len(EARLY)
    acc[0 : n * 8, :] = early_ref[...].reshape(n * 8, 128)
    for pairs in (LATE, *CROSS):
        for p, total in enumerate(products(load, pairs, groups)):
            acc[(n + p) * 8 : (n + p) * 8 + 8, :] = total
        n += len(pairs)
    acc[n * 8 :, :] = jnp.zeros((SLOTS * 8 - n * 8, 128), jnp.float32)
    by_lane = acc[pl.ds(0, SLOTS, stride=8), :]
    for s in range(1, 8):
        by_lane = by_lane + acc[pl.ds(s, SLOTS, stride=8), :]
    total = lax.dot_general(
        jnp.ones((8, 128), jnp.float32), by_lane, (((1,), (1,)), ((), ())),
        precision=lax.Precision.HIGHEST, preferred_element_type=jnp.float32,
    )
    second = jnp.concatenate([total[:, 128:], jnp.zeros((8, 256 - SLOTS), jnp.float32)], axis=1)
    even = lax.broadcasted_iota(jnp.int32, (8, 128), 0) % 2 == 0
    both = jnp.where(even, total[:, :128], second)
    for k in range(sums_ref.shape[0] // 8):
        sums_ref[k * 8 : k * 8 + 8, :] = both


def combine_kernel(
    count, chunks,
    sums_ref, first_ref, second_ref, start_ref, basis_ref, prior_ref,
    new_hbm, coeffs_ref,
    new, spread, out_sems,
):
    wx, wy = start_ref.shape[0], start_ref.shape[1]
    part = wx // chunks
    total = sums_ref[0:8, :]
    for k in range(1, sums_ref.shape[0] // 8):
        total = total + sums_ref[k * 8 : k * 8 + 8, :]
    total = total + pltpu.roll(total, 4, 0)
    total = (total + pltpu.roll(total, 2, 0)) * (1.0 / count)
    flat = jnp.concatenate([total[0:1, :], total[1:2, :]], axis=1)
    contract = functools.partial(
        lax.dot_general, dimension_numbers=(((1,), (1,)), ((), ())),
        precision=lax.Precision.HIGHEST, preferred_element_type=jnp.float32,
    )
    first, second = first_ref[...], second_ref[...]
    full = contract(first[:24] * flat, second) + contract(second[:24] * flat, first)
    top, low = full[0:8, :], full[8:24, :]
    inner = 2.0 * top
    for k in range(PRIOR):
        inner = inner - top[:, k : k + 1] * top[k : k + 1, :]
    gram = low
    for k in range(PRIOR):
        gram = gram - low[:, k : k + 1] * inner[k : k + 1, :]
    lane = lax.broadcasted_iota(jnp.int32, (16, 128), 1)
    row = lax.broadcasted_iota(jnp.int32, (16, 128), 0)
    work = jnp.where(lane < NEW, pltpu.roll(gram, 128 - PRIOR, 1), 0.0)
    work = work + jnp.where(lane == row + 16, 1.0, 0.0)
    work = work + jnp.where((lane >= 32) & (lane < 32 + PRIOR), pltpu.roll(low, 32, 1), 0.0)
    for k in range(NEW):
        pivot = work[k : k + 1, k : k + 1]
        scaled = work[k : k + 1, :] / jnp.sqrt(pivot)
        column = work[:, k : k + 1] / pivot
        work = jnp.where(row > k, work - column * work[k : k + 1, :], jnp.where(row == k, scaled, work))
    upper = jnp.where((lane >= row) & (lane < NEW), work, 0.0)
    both = jnp.concatenate([pltpu.roll(top, 128 - PRIOR, 1), upper], axis=0)
    both = jnp.concatenate([both, jnp.zeros((104, 128), jnp.float32)], axis=0)
    coeffs_ref[...] = both.T[:NEW, :FIELDS]
    for i in range(FIELDS):
        at = 16 + i if i < NEW else 32 + i - NEW
        spread[i] = jnp.broadcast_to(work[:, at : at + 1], (16, 128))

    stores = []
    for k in range(chunks):
        def some(g, carry, k=k):
            x, y = k * part + g // (wy // 16), g % (wy // 16)
            ys = pl.ds(pl.multiple_of(y * 16, 16), 16)
            tiles = [start_ref[x, ys, :]] + [basis_ref[i, x, ys, :] for i in range(STEPS)]
            tiles += [prior_ref[i, x, ys, :] for i in range(PRIOR)]
            for j in range(NEW):
                r = spread[0, j : j + 1, :] * tiles[0]
                for i in range(1, j + 1):
                    r = r + spread[i, j : j + 1, :] * tiles[i]
                for i in range(NEW, FIELDS):
                    r = r - spread[i, j : j + 1, :] * tiles[i]
                new[j, x, ys, :] = r
            return carry

        lax.fori_loop(0, part * (wy // 16), some, 0)
        xs = pl.ds(k * part, part)
        stores.append(pltpu.make_async_copy(new.at[:, xs], new_hbm.at[:, xs], out_sems.at[k]))
        stores[-1].start()
    for c in stores:
        c.wait()


def on_device(start, velocity, prior, shifts):
    wx, wy, wz = start.shape
    nx, ny = lax.axis_size("gx"), lax.axis_size("gy")
    devices = nx * ny
    ahead_x, ahead_y = ([(i, i + 1) for i in range(n - 1)] for n in (nx, ny))
    back_x, back_y = ([(i + 1, i) for i in range(n - 1)] for n in (nx, ny))

    f32 = jnp.float32
    vmem = pl.BlockSpec(memory_space=pltpu.VMEM)
    smem = pl.BlockSpec(memory_space=pltpu.SMEM)
    hbm = pl.BlockSpec(memory_space=pl.ANY)
    limit = pltpu.CompilerParams(vmem_limit_bytes=32 * 1024 * 1024)
    edge_y = jax.ShapeDtypeStruct((4, wx, H, wz), f32)
    edge_x = jax.ShapeDtypeStruct((4, H, wy, wz), f32)
    corner = jax.ShapeDtypeStruct((CORNER, wz), f32)
    start_hbm, velocity_hbm, prior_hbm = (
        pltpu.with_memory_space_constraint(v, pltpu.HBM) for v in (start, velocity, prior)
    )
    y_first, y_last, x_first, x_last = pl.pallas_call(
        pack_kernel,
        out_shape=(edge_y, edge_y, edge_x, edge_x),
        in_specs=[hbm, hbm],
        out_specs=(vmem,) * 4,
        scratch_shapes=[pltpu.SemaphoreType.DMA((8,))],
        compiler_params=limit,
        name="pack",
    )(start_hbm, velocity_hbm)
    xl = lax.ppermute(x_last, "gx", ahead_x)
    xh = lax.ppermute(x_first, "gx", back_x)
    yl = lax.ppermute(y_last, "gy", ahead_y)
    yh = lax.ppermute(y_first, "gy", back_y)
    to_up, to_down = pl.pallas_call(
        corner_kernel,
        out_shape=(corner, corner),
        in_specs=[vmem, vmem],
        out_specs=(vmem, vmem),
        compiler_params=limit,
        name="corner",
    )(xl, xh)
    cl = lax.ppermute(to_up, "gy", ahead_y)
    ch = lax.ppermute(to_down, "gy", back_y)
    early, prior_in, start_in = pl.pallas_call(
        early_kernel,
        out_shape=(
            jax.ShapeDtypeStruct((len(EARLY), 8, 128), f32),
            pltpu.VMEM(prior.shape, f32),
            pltpu.VMEM(start.shape, f32),
        ),
        in_specs=[hbm, hbm],
        out_specs=(vmem, vmem, vmem),
        scratch_shapes=[pltpu.SemaphoreType.DMA((4, 2))],
        compiler_params=limit,
        name="early",
    )(prior_hbm, start_hbm)
    ix, iy = lax.axis_index("gx"), lax.axis_index("gy")
    sides = jnp.stack([ix > 0, ix < nx - 1, iy > 0, iy < ny - 1]).astype(jnp.float32)

    ex, ey = wx + 2 * H, wy + 4 * H
    basis, sums = pl.pallas_call(
        stencil_kernel,
        out_shape=(
            pltpu.VMEM((STEPS, wx, wy, wz), f32),
            jax.ShapeDtypeStruct((devices * 2, 128), f32),
        ),
        in_specs=[smem, smem, vmem] + [hbm] * 5 + [vmem] * 4,
        out_specs=(vmem, vmem),
        scratch_shapes=[
            pltpu.VMEM((4, ex, ey, wz), f32),
            pltpu.VMEM((ex, ey, wz), f32),
            pltpu.VMEM((ex, ey, wz), f32),
            pltpu.VMEM((SLOTS * 8, 128), f32),
            pltpu.SemaphoreType.DMA((6,)),
        ],
        compiler_params=limit,
        name="stencil",
    )(shifts, sides, start_in, velocity_hbm, yl, yh, xl, xh, cl, ch, prior_in, early)
    every = lax.all_to_all(sums, AXES, 0, 0, tiled=True)
    chunks = 4
    first, second = pair_tables()
    basis_new, coeffs = pl.pallas_call(
        functools.partial(combine_kernel, float(devices * wx * wy * wz), chunks),
        out_shape=(
            jax.ShapeDtypeStruct((NEW, wx, wy, wz), f32),
            jax.ShapeDtypeStruct((NEW, FIELDS), f32),
        ),
        in_specs=[vmem] * 6,
        out_specs=(hbm, vmem),
        scratch_shapes=[
            pltpu.VMEM((NEW, wx, wy, wz), f32),
            pltpu.VMEM((FIELDS, 16, 128), f32),
            pltpu.SemaphoreType.DMA((chunks,)),
        ],
        compiler_params=limit,
        name="combine",
    )(every, jnp.asarray(first), jnp.asarray(second), start_in, basis, prior_in)
    return basis_new, coeffs.T


def solution(mesh):
    return jax.shard_map(
        on_device,
        mesh=mesh,
        in_specs=(P("gx", "gy", None), P(None, "gx", "gy", None), P(None, "gx", "gy", None), P()),
        out_specs=(P(None, "gx", "gy", None), P()),
        check_vma=False,
    )
```

```python
import functools

import jax
import jax.numpy as jnp
import numpy as np
from jax import lax
from jax.experimental import pallas as pl
from jax.experimental.pallas import tpu as pltpu
from jax.sharding import PartitionSpec as P

STEPS = 8
PRIOR = 8
NEW = STEPS + 1
FIELDS = PRIOR + NEW
H = STEPS
DRIFT = 0.3
SIXTH = 1.0 / 6.0
AXES = ("gx", "gy")

EARLY = [(i, j) for i in range(9) for j in range(i, 9)]
LATE = [(i, j) for i in range(9, 17) for j in range(i, 17)]
CROSS = [[(i, j) for i in range(9) for j in range(lo, lo + 4)] for lo in (9, 13)]
PAIRS = EARLY + LATE + CROSS[0] + CROSS[1]
SLOTS = 160


def pair_tables():
    first = np.zeros((128, 256), np.float32)
    second = np.zeros((128, 256), np.float32)
    for p, (i, j) in enumerate(PAIRS):
        first[i, p] = 0.5 if i == j else 1.0
        second[j, p] = 1.0
    return first, second


def corner_rows():
    at, pieces = 0, []
    for d in range(1, H):
        for f in range(4):
            n = H - d if f == 0 else H - 1 - d
            if n:
                pieces.append((at, d, f, n))
            at += n
    return pieces


CORNER = 2 * sum(n for _, _, _, n in corner_rows())


def pack_kernel(place_ref, start_ref, vel_ref, y_even, y_odd, x_even, x_odd, sems):
    wx, wy = start_ref.shape[0], start_ref.shape[1]
    full = slice(None)
    odd_x, odd_y = place_ref[4], place_ref[5]

    def cut(n, odd):
        return pl.ds(pl.multiple_of((n - H) * odd, H), H)

    copies = []
    for out, where in (
        (x_odd, (cut(wx, odd_x), full)),
        (x_even, (cut(wx, 1 - odd_x), full)),
        (y_odd, (full, cut(wy, odd_y))),
        (y_even, (full, cut(wy, 1 - odd_y))),
    ):
        copies.append((start_ref.at[where], out.at[0]))
        copies.append((vel_ref.at[(full, *where)], out.at[pl.ds(1, 3)]))
    copies = [pltpu.make_async_copy(src, dst, sems.at[k]) for k, (src, dst) in enumerate(copies)]
    for c in copies:
        c.start()
    for c in copies:
        c.wait()


def corner_kernel(place_ref, xe_ref, xo_ref, even_ref, odd_ref):
    wy = xe_ref.shape[2]
    odd_x, odd_y = place_ref[4] == 1, place_ref[5] == 1

    def put(at, f, row, n, low):
        for_low, for_high = (xe_ref, xo_ref) if low else (xo_ref, xe_ref)
        last = jnp.where(odd_x, for_low[f, row, wy - n :, :], for_high[f, row, wy - n :, :])
        first = jnp.where(odd_x, for_low[f, row, :n, :], for_high[f, row, :n, :])
        even_ref[at : at + n, :] = jnp.where(odd_y, first, last)
        odd_ref[at : at + n, :] = jnp.where(odd_y, last, first)

    for at, d, f, n in corner_rows():
        put(at, f, H - d, n, True)
        put(at + CORNER // 2, f, d - 1, n, False)


def products(load, pairs, groups, start=None):
    used = sorted({f for pair in pairs for f in pair})

    def body(g, totals):
        tile = {f: load(f, g) for f in used}
        return tuple(t + tile[i] * tile[j] for t, (i, j) in zip(totals, pairs))

    if start is None:
        start = (jnp.zeros((8, 128), jnp.float32),) * len(pairs)
    return lax.fori_loop(0, groups, body, start, unroll=8)


def early_kernel(prior_hbm, start_hbm, vel_hbm, out_ref, prior_ref, field, flow, sems):
    wx, wy = prior_ref.shape[1], prior_ref.shape[2]
    blocks = wy // 8
    parts = sems.shape[0] - 1
    part = wx // parts
    copies = []
    for k in range(parts):
        xs = pl.ds(k * part, part)
        inside = field.at[pl.ds(H + k * part, part), pl.ds(H, wy)]
        copies.append([
            pltpu.make_async_copy(prior_hbm.at[:, xs], prior_ref.at[:, xs], sems.at[k, 0]),
            pltpu.make_async_copy(start_hbm.at[xs], inside, sems.at[k, 1]),
        ])
        for c in copies[-1]:
            c.start()
    last = pltpu.make_async_copy(vel_hbm, flow.at[:, pl.ds(H, wx)], sems.at[parts, 0])
    last.start()

    totals = None
    for k in range(parts):
        for c in copies[k]:
            c.wait()

        def load(f, g, k=k):
            x, y = k * part + g // blocks, g % blocks * 8
            if f < 8:
                return prior_ref[f, x, pl.ds(pl.multiple_of(y, 8), 8), :]
            return field[H + x, pl.ds(pl.multiple_of(H + y, 8), 8), :]

        totals = products(load, EARLY, part * blocks, totals)
    for p, total in enumerate(totals):
        out_ref[p] = total
    last.wait()


def side(low, near, far):
    return pl.ds(pl.multiple_of(far - low * (far - near), H), H)


def coefficients(flow):
    lane = lax.broadcasted_iota(jnp.int32, (1, 1, 128), 2)
    a2 = DRIFT * flow[2]
    up = jnp.where(lane < 127, a2 - SIXTH, 0.0)
    down = jnp.where(lane > 0, -a2 - SIXTH, 0.0)
    return DRIFT * flow[0], DRIFT * flow[1], up, down


def stepped(src, x, n, y, size, keep, coefficient):
    here, ys = pl.ds(x, n), pl.ds(y, size)
    c = src[here, ys, :]
    e, w = src[pl.ds(x + 1, n), ys, :], src[pl.ds(x - 1, n), ys, :]
    u, d = src[here, pl.ds(y + 1, size), :], src[here, pl.ds(y - 1, size), :]
    a0, a1, up, down = coefficient
    above, below = pltpu.roll(c, 127, 2), pltpu.roll(c, 1, 2)
    return keep * c - SIXTH * ((e + w) + (u + d)) + a0 * (e - w) + a1 * (u - d) + (up * above + down * below)


def over_x(step, wx, rows, scale_low, scale_high, ready=None):
    def some(n):
        def body(i, carry):
            for k in range(0, n, 2):
                rows(H + (2 if ready else 0) + i * n + k, 2, None)
            return carry

        return body

    if ready:
        lax.fori_loop(0, 2, some(wx // 2 - 2), 0)
        ready()
        rows(H, 2, None)
        rows(H + wx - 2, 2, None)
    halo = STEPS - 1 - step
    for k in range(0, halo, 2):
        n = min(2, halo - k)
        rows(H - halo + k, n, scale_low)
        rows(H + wx + k, n, scale_high)
    if not ready:
        lax.fori_loop(0, wx // 16, some(16), 0)


def late_products(fields, prior_ref, wx, blocks, acc, start):
    count = len(blocks)
    gap = blocks[1] - blocks[0]

    def load(f, g):
        x, y = g // count, blocks[0] * 8 + g % count * (gap * 8)
        if f < 8:
            return prior_ref[f, x, pl.ds(pl.multiple_of(y, 8), 8), :]
        return fields[f - 8][H + x, pl.ds(pl.multiple_of(H + y, 8), 8), :]

    n = len(EARLY)
    for pairs in (LATE, *CROSS):
        before = None
        if not start:
            before = tuple(acc[(n + p) * 8 : (n + p) * 8 + 8, :] for p in range(len(pairs)))
        for p, total in enumerate(products(load, pairs, wx * count, before)):
            acc[(n + p) * 8 : (n + p) * 8 + 8, :] = total
        n += len(pairs)


def inner_kernel(
    shifts_ref, place_ref, xe_ref, xo_ref, prior_ref, early_ref, field_in, flow_in, *rest
):
    fields, (flow, low, high, acc, coef, sems) = rest[:NEW], rest[NEW:]
    wx, wy = prior_ref.shape[1], prior_ref.shape[2]
    mid_y = pl.ds(H, wy)
    odd_x = place_ref[4]
    even_at, odd_at = side(odd_x, 0, H + wx), side(1 - odd_x, 0, H + wx)
    copies = [
        (xe_ref.at[0], fields[0].at[even_at, mid_y]),
        (xo_ref.at[0], fields[0].at[odd_at, mid_y]),
        (xe_ref.at[pl.ds(1, 3)], flow.at[:, even_at]),
        (xo_ref.at[pl.ds(1, 3)], flow.at[:, odd_at]),
    ]
    copies = [pltpu.make_async_copy(src, dst, sems.at[k]) for k, (src, dst) in enumerate(copies)]
    for c in copies:
        c.start()
    n = len(EARLY)
    acc[0 : n * 8, :] = early_ref[...].reshape(n * 8, 128)

    def ready():
        for c in copies:
            c.wait()

    x_low, x_high = (place_ref[k].astype(jnp.float32) for k in range(2))
    for step in range(STEPS):
        keep = 1.0 - shifts_ref[step]
        skip = 0 if step < 3 else 4 if step < 7 else 8

        def rows(x, n, scale, step=step, keep=keep, skip=skip):
            here, size = pl.ds(x, n), wy - 2 * skip
            if step == 0:
                cs = coefficients([flow[k, here, :, :] for k in range(3)])
                for k in range(4):
                    coef[k, here, :, :] = cs[k]
                    low[k, here, H:, :] = cs[k][:, :H]
                    high[k, here, :H, :] = cs[k][:, wy - H :]
            else:
                cs = [coef[k, here, pl.ds(skip, size), :] for k in range(4)]
            r = stepped(fields[step], x, n, H + skip, size, keep, cs)
            fields[step + 1][here, pl.ds(H + skip, size), :] = r if scale is None else r * scale

        over_x(step, wx, rows, x_low, x_high, ready if step == 0 else None)
    late_products(fields, prior_ref, wx, range(1, wy // 8 - 1), acc, True)


def outer_kernel(
    shifts_ref, place_ref, yo_ref, ye_ref, co_ref, ce_ref, prior_ref, acc_ref, *rest
):
    low, high, *fields = rest[NEW + 2 : 2 * NEW + 4]
    sums_ref, flow, acc, sems = rest[2 * NEW + 4 :]
    wx, wy = prior_ref.shape[1], prior_ref.shape[2]
    mid_x = pl.ds(H, wx)
    odd_y = place_ref[5]
    copies = []
    for ref, first in ((ye_ref, odd_y), (yo_ref, 1 - odd_y)):
        copies.append((ref.at[0], fields[0].at[mid_x, side(first, 0, H + wy)]))
        copies.append((ref.at[pl.ds(1, 3)], flow.at[:, mid_x, side(first, 0, H)]))
    copies = [pltpu.make_async_copy(src, dst, sems.at[k]) for k, (src, dst) in enumerate(copies)]
    for c in copies:
        c.start()
    acc[...] = acc_ref[...]
    for at, d, f, n in corner_rows():
        for x in (H - d, H + wx - 1 + d):
            even, odd = ce_ref[at : at + n, :], co_ref[at : at + n, :]
            ahead, behind = jnp.where(odd_y == 1, even, odd), jnp.where(odd_y == 1, odd, even)
            if f == 0:
                fields[0][x, H - n : H, :] = ahead
                fields[0][x, H + wy : H + wy + n, :] = behind
            else:
                flow[f - 1, x, H - n : H, :] = ahead
                flow[f - 1, x, H : H + n, :] = behind
            at += CORNER // 2
    for c in copies:
        c.wait()

    def prepare(i, carry):
        for m in range(0, 16, 2):
            here = pl.ds(i * 16 + m, 2)
            for out, ys in ((low, pl.ds(0, H)), (high, pl.ds(H, H))):
                for k, c in enumerate(coefficients([flow[k, here, ys, :] for k in range(3)])):
                    out[k, here, ys, :] = c
        return carry

    lax.fori_loop(0, (wx + 2 * H) // 16, prepare, 0)
    x_low, x_high, y_low, y_high = (place_ref[k].astype(jnp.float32) for k in range(4))
    row = lax.broadcasted_iota(jnp.int32, (1, 8, 128), 1)
    for step in range(STEPS):
        keep = 1.0 - shifts_ref[step]
        windows = (
            (H + step - 7, low, step + 1, jnp.where(row < 7 - step, y_low, 1.0)),
            (H + wy - 1 - step, high, 7 - step, jnp.where(row > step, y_high, 1.0)),
        )

        def rows(x, n, scale, step=step, keep=keep, windows=windows):
            here = pl.ds(x, n)
            for at, coef, first, inside in windows:
                cs = [coef[k, here, pl.ds(first, 8), :] for k in range(4)]
                r = stepped(fields[step], x, n, at, 8, keep, cs)
                if step < STEPS - 1:
                    r = r * (inside if scale is None else inside * scale)
                fields[step + 1][here, pl.ds(at, 8), :] = r

        over_x(step, wx, rows, x_low, x_high)
    late_products(fields, prior_ref, wx, (0, wy // 8 - 1), acc, False)
    n = len(PAIRS)
    acc[n * 8 :, :] = jnp.zeros((SLOTS * 8 - n * 8, 128), jnp.float32)
    by_lane = acc[pl.ds(0, SLOTS, stride=8), :]
    for s in range(1, 8):
        by_lane = by_lane + acc[pl.ds(s, SLOTS, stride=8), :]
    total = lax.dot_general(
        jnp.ones((8, 128), jnp.float32), by_lane, (((1,), (1,)), ((), ())),
        precision=lax.Precision.HIGHEST, preferred_element_type=jnp.float32,
    )
    second = jnp.concatenate([total[:, 128:], jnp.zeros((8, 256 - SLOTS), jnp.float32)], axis=1)
    even = lax.broadcasted_iota(jnp.int32, (8, 128), 0) % 2 == 0
    both = jnp.where(even, total[:, :128], second)
    sums_ref[...] = both


def combine_kernel(
    count, chunks, sums_ref, first_ref, second_ref, prior_ref, *rest
):
    fields, (new_hbm, coeffs_ref, new, spread, out_sems) = rest[:NEW], rest[NEW:]
    wx, wy = prior_ref.shape[1], prior_ref.shape[2]
    part = wx // chunks
    total = sums_ref[0:8, :]
    for k in range(1, sums_ref.shape[0] // 8):
        total = total + sums_ref[k * 8 : k * 8 + 8, :]
    total = total + pltpu.roll(total, 4, 0)
    total = (total + pltpu.roll(total, 2, 0)) * (1.0 / count)
    flat = jnp.concatenate([total[0:1, :], total[1:2, :]], axis=1)
    contract = functools.partial(
        lax.dot_general, dimension_numbers=(((1,), (1,)), ((), ())),
        precision=lax.Precision.HIGHEST, preferred_element_type=jnp.float32,
    )
    first, second = first_ref[...], second_ref[...]
    full = contract(first[:24] * flat, second) + contract(second[:24] * flat, first)
    top, low = full[0:8, :], full[8:24, :]
    inner = 2.0 * top
    for k in range(PRIOR):
        inner = inner - top[:, k : k + 1] * top[k : k + 1, :]
    gram = low
    for k in range(PRIOR):
        gram = gram - low[:, k : k + 1] * inner[k : k + 1, :]
    lane = lax.broadcasted_iota(jnp.int32, (16, 128), 1)
    row = lax.broadcasted_iota(jnp.int32, (16, 128), 0)
    work = jnp.where(lane < NEW, pltpu.roll(gram, 128 - PRIOR, 1), 0.0)
    work = work + jnp.where(lane == row + 16, 1.0, 0.0)
    work = work + jnp.where((lane >= 32) & (lane < 32 + PRIOR), pltpu.roll(low, 32, 1), 0.0)
    for k in range(NEW):
        pivot = work[k : k + 1, k : k + 1]
        scaled = work[k : k + 1, :] / jnp.sqrt(pivot)
        column = work[:, k : k + 1] / pivot
        work = jnp.where(row > k, work - column * work[k : k + 1, :], jnp.where(row == k, scaled, work))
    upper = jnp.where((lane >= row) & (lane < NEW), work, 0.0)
    both = jnp.concatenate([pltpu.roll(top, 128 - PRIOR, 1), upper], axis=0)
    both = jnp.concatenate([both, jnp.zeros((104, 128), jnp.float32)], axis=0)
    coeffs_ref[...] = both.T[:NEW, :FIELDS]
    for i in range(FIELDS):
        at = 16 + i if i < NEW else 32 + i - NEW
        spread[i] = jnp.broadcast_to(work[:, at : at + 1], (16, 128))

    stores = []
    for k in range(chunks):
        def some(g, carry, k=k):
            x, y = k * part + g // (wy // 16), g % (wy // 16)
            ys = pl.ds(pl.multiple_of(y * 16, 16), 16)
            inner = pl.ds(pl.multiple_of(H + y * 16, 8), 16)
            tiles = [fields[i][H + x, inner, :] for i in range(NEW)]
            tiles += [prior_ref[i, x, ys, :] for i in range(PRIOR)]
            for j in range(NEW):
                r = spread[0, j : j + 1, :] * tiles[0]
                for i in range(1, j + 1):
                    r = r + spread[i, j : j + 1, :] * tiles[i]
                for i in range(NEW, FIELDS):
                    r = r - spread[i, j : j + 1, :] * tiles[i]
                new[j, x, ys, :] = r
            return carry

        lax.fori_loop(0, part * (wy // 16), some, 0, unroll=2)
        xs = pl.ds(k * part, part)
        stores.append(pltpu.make_async_copy(new.at[:, xs], new_hbm.at[:, xs], out_sems.at[k]))
        stores[-1].start()
    for c in stores:
        c.wait()


def on_device(start, velocity, prior, shifts):
    wx, wy, wz = start.shape
    nx, ny = lax.axis_size("gx"), lax.axis_size("gy")
    devices = nx * ny
    swaps = {
        axis: [[pair for i in range(odd, n - 1, 2) for pair in ((i, i + 1), (i + 1, i))] for odd in (0, 1)]
        for axis, n in (("gx", nx), ("gy", ny))
    }
    ix, iy = lax.axis_index("gx"), lax.axis_index("gy")
    place = jnp.stack([ix > 0, ix < nx - 1, iy > 0, iy < ny - 1, ix % 2 == 1, iy % 2 == 1]).astype(jnp.int32)

    f32 = jnp.float32
    vmem = pl.BlockSpec(memory_space=pltpu.VMEM)
    smem = pl.BlockSpec(memory_space=pltpu.SMEM)
    hbm = pl.BlockSpec(memory_space=pl.ANY)
    limit = pltpu.CompilerParams(vmem_limit_bytes=12 * 1024 * 1024)
    edge_y = jax.ShapeDtypeStruct((4, wx, H, wz), f32)
    edge_x = jax.ShapeDtypeStruct((4, H, wy, wz), f32)
    corner = jax.ShapeDtypeStruct((CORNER, wz), f32)
    start_hbm, velocity_hbm, prior_hbm = (
        pltpu.with_memory_space_constraint(v, pltpu.HBM) for v in (start, velocity, prior)
    )
    y_even, y_odd, x_even, x_odd = pl.pallas_call(
        pack_kernel,
        out_shape=(edge_y, edge_y, edge_x, edge_x),
        in_specs=[smem, hbm, hbm],
        out_specs=(vmem,) * 4,
        scratch_shapes=[pltpu.SemaphoreType.DMA((8,))],
        compiler_params=limit,
        name="pack",
    )(place, start_hbm, velocity_hbm)
    xo = lax.ppermute(x_odd, "gx", swaps["gx"][1])
    xe = lax.ppermute(x_even, "gx", swaps["gx"][0])
    yo = lax.ppermute(y_odd, "gy", swaps["gy"][1])
    ye = lax.ppermute(y_even, "gy", swaps["gy"][0])
    ex, ey = wx + 2 * H, wy + 2 * H
    field = pltpu.VMEM((ex, ey, wz), f32)
    flow = pltpu.VMEM((3, ex, wy, wz), f32)
    strip = pltpu.VMEM((4, ex, 2 * H, wz), f32)
    early, prior_in, first, flows = pl.pallas_call(
        early_kernel,
        out_shape=(
            jax.ShapeDtypeStruct((len(EARLY), 8, 128), f32),
            pltpu.VMEM(prior.shape, f32),
            field,
            flow,
        ),
        in_specs=[hbm] * 3,
        out_specs=(vmem,) * 4,
        scratch_shapes=[pltpu.SemaphoreType.DMA((9, 2))],
        compiler_params=limit,
        name="early",
    )(prior_hbm, start_hbm, velocity_hbm)
    xe, xo, early = lax.optimization_barrier((xe, xo, early))
    c_even, c_odd = pl.pallas_call(
        corner_kernel,
        out_shape=(corner, corner),
        in_specs=[smem, vmem, vmem],
        out_specs=(vmem, vmem),
        compiler_params=limit,
        name="corner",
    )(place, xe, xo)
    co = lax.ppermute(c_odd, "gy", swaps["gy"][1])
    ce = lax.ppermute(c_even, "gy", swaps["gy"][0])
    *fields, flows, low, high, acc = pl.pallas_call(
        inner_kernel,
        out_shape=(*[field] * NEW, flow, strip, strip, pltpu.VMEM((SLOTS * 8, 128), f32)),
        in_specs=[smem, smem, hbm, hbm] + [vmem] * 4,
        out_specs=(vmem,) * (NEW + 4),
        scratch_shapes=[pltpu.VMEM((4, ex, wy, wz), f32), pltpu.SemaphoreType.DMA((4,))],
        input_output_aliases={6: 0, 7: NEW},
        compiler_params=limit,
        name="inner",
    )(shifts, place, xe, xo, prior_in, early, first, flows)
    low, high, *fields, sums = pl.pallas_call(
        outer_kernel,
        out_shape=(strip, strip, *[field] * NEW, jax.ShapeDtypeStruct((8, 128), f32)),
        in_specs=[smem, smem, hbm, hbm] + [vmem] * (6 + NEW),
        out_specs=(vmem,) * (NEW + 3),
        scratch_shapes=[
            pltpu.VMEM((3, ex, 2 * H, wz), f32),
            pltpu.VMEM((SLOTS * 8, 128), f32),
            pltpu.SemaphoreType.DMA((4,)),
        ],
        input_output_aliases={8 + k: k for k in range(NEW + 2)},
        compiler_params=limit,
        name="outer",
    )(shifts, place, yo, ye, co, ce, prior_in, acc, low, high, *fields)
    sums = sums + lax.ppermute(sums, "gx", swaps["gx"][0])
    chips = devices // 2
    cores = [[x * ny + y for x in range(core, nx, 2) for y in range(ny)] for core in (0, 1)]
    sums = jnp.broadcast_to(sums[None], (chips // 4, 8, 128)).reshape(chips * 2, 128)
    every = lax.all_to_all(sums, AXES, 0, 0, tiled=True, axis_index_groups=cores)
    chunks = 8
    first, second = pair_tables()
    basis_new, coeffs = pl.pallas_call(
        functools.partial(combine_kernel, float(devices * wx * wy * wz), chunks),
        out_shape=(
            jax.ShapeDtypeStruct((NEW, wx, wy, wz), f32),
            jax.ShapeDtypeStruct((NEW, FIELDS), f32),
        ),
        in_specs=[vmem] * (4 + NEW),
        out_specs=(hbm, vmem),
        scratch_shapes=[
            pltpu.VMEM((NEW, wx, wy, wz), f32),
            pltpu.VMEM((FIELDS, 16, 128), f32),
            pltpu.SemaphoreType.DMA((chunks,)),
        ],
        compiler_params=limit,
        name="combine",
    )(every, jnp.asarray(first), jnp.asarray(second), prior_in, *fields)
    return basis_new, coeffs.T


def solution(mesh):
    return jax.shard_map(
        on_device,
        mesh=mesh,
        in_specs=(P("gx", "gy", None), P(None, "gx", "gy", None), P(None, "gx", "gy", None), P()),
        out_specs=(P(None, "gx", "gy", None), P()),
        check_vma=False,
    )
```

```python
import functools

import jax
import jax.numpy as jnp
import numpy as np
from jax import lax
from jax.experimental import pallas as pl
from jax.experimental.pallas import tpu as pltpu
from jax.sharding import PartitionSpec as P

STEPS = 8
PRIOR = 8
NEW = STEPS + 1
FIELDS = PRIOR + NEW
H = STEPS
DRIFT = 0.3
SIXTH = 1.0 / 6.0
AXES = ("gx", "gy")

EARLY = [(i, j) for i in range(9) for j in range(i, 9)]
LATE = [(i, j) for i in range(9, 17) for j in range(i, 17)]
CROSS = [[(i, j) for i in range(9) for j in range(lo, lo + 4)] for lo in (9, 13)]
PAIRS = EARLY + LATE + CROSS[0] + CROSS[1]
SLOTS = 160


def pair_tables():
    first = np.zeros((128, 256), np.float32)
    second = np.zeros((128, 256), np.float32)
    for p, (i, j) in enumerate(PAIRS):
        first[i, p] = 0.5 if i == j else 1.0
        second[j, p] = 1.0
    return first, second


def corner_rows():
    at, pieces = 0, []
    for d in range(1, H):
        for f in range(4):
            n = H - d if f == 0 else H - 1 - d
            if n:
                pieces.append((at, d, f, n))
            at += n
    return pieces


CORNER = 2 * sum(n for _, _, _, n in corner_rows())


def pack_kernel(place_ref, start_ref, vel_ref, y_even, y_odd, x_even, x_odd, sems):
    wx, wy = start_ref.shape[0], start_ref.shape[1]
    full = slice(None)
    odd_x, odd_y = place_ref[4], place_ref[5]

    def cut(n, odd):
        return pl.ds(pl.multiple_of((n - H) * odd, H), H)

    copies = []
    for out, where in (
        (x_odd, (cut(wx, odd_x), full)),
        (x_even, (cut(wx, 1 - odd_x), full)),
        (y_odd, (full, cut(wy, odd_y))),
        (y_even, (full, cut(wy, 1 - odd_y))),
    ):
        copies.append((start_ref.at[where], out.at[0]))
        copies.append((vel_ref.at[(full, *where)], out.at[pl.ds(1, 3)]))
    copies = [pltpu.make_async_copy(src, dst, sems.at[k]) for k, (src, dst) in enumerate(copies)]
    for c in copies:
        c.start()
    for c in copies:
        c.wait()


def corner_kernel(place_ref, xe_ref, xo_ref, even_ref, odd_ref):
    wy = xe_ref.shape[2]
    odd_x, odd_y = place_ref[4] == 1, place_ref[5] == 1

    def put(at, f, row, n, low):
        for_low, for_high = (xe_ref, xo_ref) if low else (xo_ref, xe_ref)
        last = jnp.where(odd_x, for_low[f, row, wy - n :, :], for_high[f, row, wy - n :, :])
        first = jnp.where(odd_x, for_low[f, row, :n, :], for_high[f, row, :n, :])
        even_ref[at : at + n, :] = jnp.where(odd_y, first, last)
        odd_ref[at : at + n, :] = jnp.where(odd_y, last, first)

    for at, d, f, n in corner_rows():
        put(at, f, H - d, n, True)
        put(at + CORNER // 2, f, d - 1, n, False)


def thirds(a):
    high = a.astype(jnp.bfloat16).astype(jnp.float32)
    rest = a - high
    middle = rest.astype(jnp.bfloat16).astype(jnp.float32)
    return high, middle, rest - middle


def products(load, pairs, groups, start=None):
    used = sorted({f for pair in pairs for f in pair})

    def body(g, totals):
        tile = {f: load(f, g) for f in used}
        return tuple(t + tile[i] * tile[j] for t, (i, j) in zip(totals, pairs))

    if start is None:
        start = (jnp.zeros((8, 128), jnp.float32),) * len(pairs)
    return lax.fori_loop(0, groups, body, start, unroll=16)


def early_kernel(prior_hbm, start_hbm, vel_hbm, out_ref, prior_ref, field, flow, sems):
    wx, wy = prior_ref.shape[1], prior_ref.shape[2]
    blocks = wy // 8
    parts = sems.shape[0] - 1
    part = wx // parts
    copies = []
    for k in range(parts):
        xs = pl.ds(k * part, part)
        inside = field.at[pl.ds(H + k * part, part), pl.ds(H, wy)]
        copies.append([
            pltpu.make_async_copy(prior_hbm.at[:, xs], prior_ref.at[:, xs], sems.at[k, 0]),
            pltpu.make_async_copy(start_hbm.at[xs], inside, sems.at[k, 1]),
        ])
        for c in copies[-1]:
            c.start()
    last = pltpu.make_async_copy(vel_hbm, flow.at[:, pl.ds(H, wx)], sems.at[parts, 0])
    last.start()

    totals = None
    for k in range(parts):
        for c in copies[k]:
            c.wait()

        def load(f, g, k=k):
            x, y = k * part + g // blocks, g % blocks * 8
            if f < 8:
                return prior_ref[f, x, pl.ds(pl.multiple_of(y, 8), 8), :]
            return field[H + x, pl.ds(pl.multiple_of(H + y, 8), 8), :]

        totals = products(load, EARLY, part * blocks, totals)
    for p, total in enumerate(totals):
        out_ref[p] = total
    last.wait()


def side(low, near, far):
    return pl.ds(pl.multiple_of(far - low * (far - near), H), H)


def coefficients(flow):
    lane = lax.broadcasted_iota(jnp.int32, (1, 1, 128), 2)
    a2 = DRIFT * flow[2]
    up = jnp.where(lane < 127, a2 - SIXTH, 0.0)
    down = jnp.where(lane > 0, -a2 - SIXTH, 0.0)
    return DRIFT * flow[0], DRIFT * flow[1], up, down


def stepped(src, x, n, y, size, keep, coefficient):
    here, ys = pl.ds(x, n), pl.ds(y, size)
    c = src[here, ys, :]
    e, w = src[pl.ds(x + 1, n), ys, :], src[pl.ds(x - 1, n), ys, :]
    u, d = src[here, pl.ds(y + 1, size), :], src[here, pl.ds(y - 1, size), :]
    a0, a1, up, down = coefficient
    above, below = pltpu.roll(c, 127, 2), pltpu.roll(c, 1, 2)
    return keep * c - SIXTH * ((e + w) + (u + d)) + a0 * (e - w) + a1 * (u - d) + (up * above + down * below)


def over_x(step, wx, rows, scale_low, scale_high, ready=None):
    def some(n):
        def body(i, carry):
            for k in range(0, n, 2):
                rows(H + (2 if ready else 0) + i * n + k, 2, None)
            return carry

        return body

    if ready:
        lax.fori_loop(0, 2, some(wx // 2 - 2), 0)
        ready()
        rows(H, 2, None)
        rows(H + wx - 2, 2, None)
    halo = STEPS - 1 - step
    for k in range(0, halo, 2):
        n = min(2, halo - k)
        rows(H - halo + k, n, scale_low)
        rows(H + wx + k, n, scale_high)
    if not ready:
        lax.fori_loop(0, wx // 16, some(16), 0)


def late_products(fields, prior_ref, wx, blocks, acc, start):
    count = len(blocks)
    gap = blocks[1] - blocks[0]

    def load(f, g):
        x, y = g // count, blocks[0] * 8 + g % count * (gap * 8)
        if f < 8:
            return prior_ref[f, x, pl.ds(pl.multiple_of(y, 8), 8), :]
        return fields[f - 8][H + x, pl.ds(pl.multiple_of(H + y, 8), 8), :]

    n = len(EARLY)
    for pairs in (LATE, *CROSS):
        before = None
        if not start:
            before = tuple(acc[(n + p) * 8 : (n + p) * 8 + 8, :] for p in range(len(pairs)))
        for p, total in enumerate(products(load, pairs, wx * count, before)):
            acc[(n + p) * 8 : (n + p) * 8 + 8, :] = total
        n += len(pairs)


def inner_kernel(
    shifts_ref, place_ref, xe_ref, xo_ref, prior_ref, early_ref, field_in, flow_in, *rest
):
    fields, (flow, low, high, acc, coef, sems) = rest[:NEW], rest[NEW:]
    wx, wy = prior_ref.shape[1], prior_ref.shape[2]
    mid_y = pl.ds(H, wy)
    odd_x = place_ref[4]
    even_at, odd_at = side(odd_x, 0, H + wx), side(1 - odd_x, 0, H + wx)
    copies = [
        (xe_ref.at[0], fields[0].at[even_at, mid_y]),
        (xo_ref.at[0], fields[0].at[odd_at, mid_y]),
        (xe_ref.at[pl.ds(1, 3)], flow.at[:, even_at]),
        (xo_ref.at[pl.ds(1, 3)], flow.at[:, odd_at]),
    ]
    copies = [pltpu.make_async_copy(src, dst, sems.at[k]) for k, (src, dst) in enumerate(copies)]
    for c in copies:
        c.start()
    n = len(EARLY)
    acc[0 : n * 8, :] = early_ref[...].reshape(n * 8, 128)

    def ready():
        for c in copies:
            c.wait()

    x_low, x_high = (place_ref[k].astype(jnp.float32) for k in range(2))
    for step in range(STEPS):
        keep = 1.0 - shifts_ref[step]
        skip = 0 if step < 3 else 4 if step < 7 else 8

        def rows(x, n, scale, step=step, keep=keep, skip=skip):
            here, size = pl.ds(x, n), wy - 2 * skip
            if step == 0:
                cs = coefficients([flow[k, here, :, :] for k in range(3)])
                for k in range(4):
                    coef[k, here, :, :] = cs[k]
                    low[k, here, H:, :] = cs[k][:, :H]
                    high[k, here, :H, :] = cs[k][:, wy - H :]
            else:
                cs = [coef[k, here, pl.ds(skip, size), :] for k in range(4)]
            r = stepped(fields[step], x, n, H + skip, size, keep, cs)
            fields[step + 1][here, pl.ds(H + skip, size), :] = r if scale is None else r * scale

        over_x(step, wx, rows, x_low, x_high, ready if step == 0 else None)
    late_products(fields, prior_ref, wx, range(1, wy // 8 - 1), acc, True)


def outer_kernel(
    shifts_ref, place_ref, yo_ref, ye_ref, co_ref, ce_ref, prior_ref, acc_ref, *rest
):
    low, high, *fields = rest[NEW + 2 : 2 * NEW + 4]
    sums_ref, flow, acc, sems = rest[2 * NEW + 4 :]
    wx, wy = prior_ref.shape[1], prior_ref.shape[2]
    mid_x = pl.ds(H, wx)
    odd_y = place_ref[5]
    copies = []
    for ref, first in ((ye_ref, odd_y), (yo_ref, 1 - odd_y)):
        copies.append((ref.at[0], fields[0].at[mid_x, side(first, 0, H + wy)]))
        copies.append((ref.at[pl.ds(1, 3)], flow.at[:, mid_x, side(first, 0, H)]))
    copies = [pltpu.make_async_copy(src, dst, sems.at[k]) for k, (src, dst) in enumerate(copies)]
    for c in copies:
        c.start()
    acc[...] = acc_ref[...]
    for at, d, f, n in corner_rows():
        for x in (H - d, H + wx - 1 + d):
            even, odd = ce_ref[at : at + n, :], co_ref[at : at + n, :]
            ahead, behind = jnp.where(odd_y == 1, even, odd), jnp.where(odd_y == 1, odd, even)
            if f == 0:
                fields[0][x, H - n : H, :] = ahead
                fields[0][x, H + wy : H + wy + n, :] = behind
            else:
                flow[f - 1, x, H - n : H, :] = ahead
                flow[f - 1, x, H : H + n, :] = behind
            at += CORNER // 2
    for c in copies:
        c.wait()

    def prepare(i, carry):
        for m in range(0, 16, 2):
            here = pl.ds(i * 16 + m, 2)
            for out, ys in ((low, pl.ds(0, H)), (high, pl.ds(H, H))):
                for k, c in enumerate(coefficients([flow[k, here, ys, :] for k in range(3)])):
                    out[k, here, ys, :] = c
        return carry

    lax.fori_loop(0, (wx + 2 * H) // 16, prepare, 0)
    x_low, x_high, y_low, y_high = (place_ref[k].astype(jnp.float32) for k in range(4))
    row = lax.broadcasted_iota(jnp.int32, (1, 8, 128), 1)
    for step in range(STEPS):
        keep = 1.0 - shifts_ref[step]
        windows = (
            (H + step - 7, low, step + 1, jnp.where(row < 7 - step, y_low, 1.0)),
            (H + wy - 1 - step, high, 7 - step, jnp.where(row > step, y_high, 1.0)),
        )

        def rows(x, n, scale, step=step, keep=keep, windows=windows):
            here = pl.ds(x, n)
            for at, coef, first, inside in windows:
                cs = [coef[k, here, pl.ds(first, 8), :] for k in range(4)]
                r = stepped(fields[step], x, n, at, 8, keep, cs)
                if step < STEPS - 1:
                    r = r * (inside if scale is None else inside * scale)
                fields[step + 1][here, pl.ds(at, 8), :] = r

        over_x(step, wx, rows, x_low, x_high)
    late_products(fields, prior_ref, wx, (0, wy // 8 - 1), acc, False)
    n = len(PAIRS)
    acc[n * 8 :, :] = jnp.zeros((SLOTS * 8 - n * 8, 128), jnp.float32)
    by_lane = acc[pl.ds(0, SLOTS, stride=8), :]
    for s in range(1, 8):
        by_lane = by_lane + acc[pl.ds(s, SLOTS, stride=8), :]
    total = lax.dot_general(
        jnp.ones((8, 3 * 128), jnp.float32), jnp.concatenate(thirds(by_lane), axis=1), (((1,), (1,)), ((), ())),
        preferred_element_type=jnp.float32,
    )
    second = jnp.concatenate([total[:, 128:], jnp.zeros((8, 256 - SLOTS), jnp.float32)], axis=1)
    even = lax.broadcasted_iota(jnp.int32, (8, 128), 0) % 2 == 0
    both = jnp.where(even, total[:, :128], second)
    sums_ref[...] = both


def combine_kernel(
    count, chunks, sums_ref, first_ref, second_ref, prior_ref, *rest
):
    fields, (new_hbm, coeffs_ref, new, spread, out_sems) = rest[:NEW], rest[NEW:]
    wx, wy = prior_ref.shape[1], prior_ref.shape[2]
    part = wx // chunks
    total = sums_ref[0:8, :]
    for k in range(1, sums_ref.shape[0] // 8):
        total = total + sums_ref[k * 8 : k * 8 + 8, :]
    total = total + pltpu.roll(total, 4, 0)
    total = (total + pltpu.roll(total, 2, 0)) * (1.0 / count)
    flat = jnp.concatenate([total[0:1, :], total[1:2, :]], axis=1)
    first, second = first_ref[:24], second_ref[:24]

    def contract(left, right):
        rows = jnp.concatenate([left * part_of for part_of in thirds(flat)], axis=0)
        r = lax.dot_general(rows, right[...], (((1,), (1,)), ((), ())), preferred_element_type=jnp.float32)
        return (r[:24] + r[24:48]) + r[48:]

    full = contract(first, second_ref) + contract(second, first_ref)
    top, low = full[0:8, :], full[8:24, :]
    inner = 2.0 * top
    for k in range(PRIOR):
        inner = inner - top[:, k : k + 1] * top[k : k + 1, :]
    gram = low
    for k in range(PRIOR):
        gram = gram - low[:, k : k + 1] * inner[k : k + 1, :]
    lane = lax.broadcasted_iota(jnp.int32, (16, 128), 1)
    row = lax.broadcasted_iota(jnp.int32, (16, 128), 0)
    columns = [jnp.broadcast_to(gram[:, PRIOR + k : PRIOR + k + 1], (16, 128)) for k in range(NEW)]
    units = [jnp.where(row == k, 1.0, 0.0) for k in range(NEW)]
    coefs = [jnp.broadcast_to(low[:, k : k + 1], (16, 128)) for k in range(PRIOR)]
    pivots = jnp.ones((16, 128), jnp.float32)
    for k in range(NEW):
        pivot = columns[k][k : k + 1, :]
        pivots = jnp.where(row == k, pivot, pivots)
        factor = jnp.where(row > k, columns[k] * (1.0 / pivot), 0.0)
        columns[k + 1 :] = [c - factor * c[k : k + 1, :] for c in columns[k + 1 :]]
        units[: k + 1] = [c - factor * c[k : k + 1, :] for c in units[: k + 1]]
        coefs = [c - factor * c[k : k + 1, :] for c in coefs]
    scale = 1.0 / jnp.sqrt(pivots)
    for i, c in enumerate(units + coefs):
        spread[i] = c * scale
    upper = jnp.zeros((16, 128), jnp.float32)
    for k in range(NEW):
        upper = jnp.where((lane == k) & (row <= k), columns[k] * scale, upper)
    both = jnp.concatenate([pltpu.roll(top, 128 - PRIOR, 1), upper], axis=0)
    stores = []
    for k in range(chunks):
        def some(g, carry, k=k):
            x, y = k * part + g // (wy // 16), g % (wy // 16)
            ys = pl.ds(pl.multiple_of(y * 16, 16), 16)
            inner = pl.ds(pl.multiple_of(H + y * 16, 8), 16)
            tiles = [fields[i][H + x, inner, :] for i in range(NEW)]
            tiles += [prior_ref[i, x, ys, :] for i in range(PRIOR)]
            for j in range(NEW):
                r = spread[0, j : j + 1, :] * tiles[0]
                for i in range(1, j + 1):
                    r = r + spread[i, j : j + 1, :] * tiles[i]
                for i in range(NEW, FIELDS):
                    r = r - spread[i, j : j + 1, :] * tiles[i]
                new[j, x, ys, :] = r
            return carry

        lax.fori_loop(0, part * (wy // 16), some, 0, unroll=2)
        xs = pl.ds(k * part, part)
        stores.append(pltpu.make_async_copy(new.at[:, xs], new_hbm.at[:, xs], out_sems.at[k]))
        stores[-1].start()
    both = jnp.concatenate([both, jnp.zeros((104, 128), jnp.float32)], axis=0)
    coeffs_ref[...] = both.T[:NEW, :FIELDS]
    for c in stores:
        c.wait()


def on_device(start, velocity, prior, shifts):
    wx, wy, wz = start.shape
    nx, ny = lax.axis_size("gx"), lax.axis_size("gy")
    devices = nx * ny
    swaps = {
        axis: [[pair for i in range(odd, n - 1, 2) for pair in ((i, i + 1), (i + 1, i))] for odd in (0, 1)]
        for axis, n in (("gx", nx), ("gy", ny))
    }
    ix, iy = lax.axis_index("gx"), lax.axis_index("gy")
    place = jnp.stack([ix > 0, ix < nx - 1, iy > 0, iy < ny - 1, ix % 2 == 1, iy % 2 == 1]).astype(jnp.int32)

    f32 = jnp.float32
    vmem = pl.BlockSpec(memory_space=pltpu.VMEM)
    smem = pl.BlockSpec(memory_space=pltpu.SMEM)
    hbm = pl.BlockSpec(memory_space=pl.ANY)
    limit = pltpu.CompilerParams(vmem_limit_bytes=12 * 1024 * 1024)
    edge_y = jax.ShapeDtypeStruct((4, wx, H, wz), f32)
    edge_x = jax.ShapeDtypeStruct((4, H, wy, wz), f32)
    corner = jax.ShapeDtypeStruct((CORNER, wz), f32)
    start_hbm, velocity_hbm, prior_hbm = (
        pltpu.with_memory_space_constraint(v, pltpu.HBM) for v in (start, velocity, prior)
    )
    y_even, y_odd, x_even, x_odd = pl.pallas_call(
        pack_kernel,
        out_shape=(edge_y, edge_y, edge_x, edge_x),
        in_specs=[smem, hbm, hbm],
        out_specs=(vmem,) * 4,
        scratch_shapes=[pltpu.SemaphoreType.DMA((8,))],
        compiler_params=limit,
        name="pack",
    )(place, start_hbm, velocity_hbm)
    xo = lax.ppermute(x_odd, "gx", swaps["gx"][1])
    xe = lax.ppermute(x_even, "gx", swaps["gx"][0])
    yo = lax.ppermute(y_odd, "gy", swaps["gy"][1])
    ye = lax.ppermute(y_even, "gy", swaps["gy"][0])
    ex, ey = wx + 2 * H, wy + 2 * H
    field = pltpu.VMEM((ex, ey, wz), f32)
    flow = pltpu.VMEM((3, ex, wy, wz), f32)
    strip = pltpu.VMEM((4, ex, 2 * H, wz), f32)
    early, prior_in, first, flows = pl.pallas_call(
        early_kernel,
        out_shape=(
            jax.ShapeDtypeStruct((len(EARLY), 8, 128), f32),
            pltpu.VMEM(prior.shape, f32),
            field,
            flow,
        ),
        in_specs=[hbm] * 3,
        out_specs=(vmem,) * 4,
        scratch_shapes=[pltpu.SemaphoreType.DMA((9, 2))],
        compiler_params=limit,
        name="early",
    )(prior_hbm, start_hbm, velocity_hbm)
    xe, xo, early = lax.optimization_barrier((xe, xo, early))
    c_even, c_odd = pl.pallas_call(
        corner_kernel,
        out_shape=(corner, corner),
        in_specs=[smem, vmem, vmem],
        out_specs=(vmem, vmem),
        compiler_params=limit,
        name="corner",
    )(place, xe, xo)
    co = lax.ppermute(c_odd, "gy", swaps["gy"][1])
    ce = lax.ppermute(c_even, "gy", swaps["gy"][0])
    *fields, flows, low, high, acc = pl.pallas_call(
        inner_kernel,
        out_shape=(*[field] * NEW, flow, strip, strip, pltpu.VMEM((SLOTS * 8, 128), f32)),
        in_specs=[smem, smem, hbm, hbm] + [vmem] * 4,
        out_specs=(vmem,) * (NEW + 4),
        scratch_shapes=[pltpu.VMEM((4, ex, wy, wz), f32), pltpu.SemaphoreType.DMA((4,))],
        input_output_aliases={6: 0, 7: NEW},
        compiler_params=limit,
        name="inner",
    )(shifts, place, xe, xo, prior_in, early, first, flows)
    low, high, *fields, sums = pl.pallas_call(
        outer_kernel,
        out_shape=(strip, strip, *[field] * NEW, jax.ShapeDtypeStruct((8, 128), f32)),
        in_specs=[smem, smem, hbm, hbm] + [vmem] * (6 + NEW),
        out_specs=(vmem,) * (NEW + 3),
        scratch_shapes=[
            pltpu.VMEM((3, ex, 2 * H, wz), f32),
            pltpu.VMEM((SLOTS * 8, 128), f32),
            pltpu.SemaphoreType.DMA((4,)),
        ],
        input_output_aliases={8 + k: k for k in range(NEW + 2)},
        compiler_params=limit,
        name="outer",
    )(shifts, place, yo, ye, co, ce, prior_in, acc, low, high, *fields)
    sums = sums + lax.ppermute(sums, "gx", swaps["gx"][0])
    chips = devices // 2
    cores = [[x * ny + y for x in range(core, nx, 2) for y in range(ny)] for core in (0, 1)]
    sums = jnp.broadcast_to(sums[None], (chips // 4, 8, 128)).reshape(chips * 2, 128)
    every = lax.all_to_all(sums, AXES, 0, 0, tiled=True, axis_index_groups=cores)
    chunks = 8
    first, second = pair_tables()
    basis_new, coeffs = pl.pallas_call(
        functools.partial(combine_kernel, float(devices * wx * wy * wz), chunks),
        out_shape=(
            jax.ShapeDtypeStruct((NEW, wx, wy, wz), f32),
            jax.ShapeDtypeStruct((NEW, FIELDS), f32),
        ),
        in_specs=[vmem] * (4 + NEW),
        out_specs=(hbm, vmem),
        scratch_shapes=[
            pltpu.VMEM((NEW, wx, wy, wz), f32),
            pltpu.VMEM((FIELDS, 16, 128), f32),
            pltpu.SemaphoreType.DMA((chunks,)),
        ],
        compiler_params=limit,
        name="combine",
    )(every, jnp.asarray(first), jnp.asarray(second), prior_in, *fields)
    return basis_new, coeffs.T


def solution(mesh):
    return jax.shard_map(
        on_device,
        mesh=mesh,
        in_specs=(P("gx", "gy", None), P(None, "gx", "gy", None), P(None, "gx", "gy", None), P()),
        out_specs=(P(None, "gx", "gy", None), P()),
        check_vma=False,
    )
```

```python
import functools

import jax
import jax.numpy as jnp
import numpy as np
from jax import lax
from jax.experimental import pallas as pl
from jax.experimental.pallas import tpu as pltpu
from jax.sharding import PartitionSpec as P

STEPS = 8
PRIOR = 8
NEW = STEPS + 1
FIELDS = PRIOR + NEW
H = STEPS
DRIFT = 0.3
SIXTH = 1.0 / 6.0
AXES = ("gx", "gy")

EARLY = [(i, j) for i in range(9) for j in range(i, 9)]
LATE = [(i, j) for i in range(9, 17) for j in range(i, 17)]
CROSS = [[(i, j) for i in range(9) for j in range(lo, lo + 4)] for lo in (9, 13)]
PAIRS = EARLY + LATE + CROSS[0] + CROSS[1]
SLOTS = 160


def pair_tables():
    first = np.zeros((128, 256), np.float32)
    second = np.zeros((128, 256), np.float32)
    for p, (i, j) in enumerate(PAIRS):
        first[i, p] = 0.5 if i == j else 1.0
        second[j, p] = 1.0
    return first, second


def corner_rows():
    at, pieces = 0, []
    for d in range(1, H):
        for f in range(4):
            n = H - d if f == 0 else H - 1 - d
            if n:
                pieces.append((at, d, f, n))
            at += n
    return pieces


CORNER = 2 * sum(n for _, _, _, n in corner_rows())


def pack_kernel(place_ref, start_ref, vel_ref, y_even, y_odd, x_even, x_odd, sems):
    wx, wy = start_ref.shape[0], start_ref.shape[1]
    full = slice(None)
    odd_x, odd_y = place_ref[4], place_ref[5]

    def cut(n, odd):
        return pl.ds(pl.multiple_of((n - H) * odd, H), H)

    copies = []
    for out, where in (
        (x_odd, (cut(wx, odd_x), full)),
        (x_even, (cut(wx, 1 - odd_x), full)),
        (y_odd, (full, cut(wy, odd_y))),
        (y_even, (full, cut(wy, 1 - odd_y))),
    ):
        copies.append((start_ref.at[where], out.at[0]))
        copies.append((vel_ref.at[(full, *where)], out.at[pl.ds(1, 3)]))
    copies = [pltpu.make_async_copy(src, dst, sems.at[k]) for k, (src, dst) in enumerate(copies)]
    for c in copies:
        c.start()
    for c in copies:
        c.wait()


def corner_kernel(place_ref, xe_ref, xo_ref, even_ref, odd_ref):
    wy = xe_ref.shape[2]
    odd_x, odd_y = place_ref[4] == 1, place_ref[5] == 1

    def put(at, f, row, n, low):
        for_low, for_high = (xe_ref, xo_ref) if low else (xo_ref, xe_ref)
        last = jnp.where(odd_x, for_low[f, row, wy - n :, :], for_high[f, row, wy - n :, :])
        first = jnp.where(odd_x, for_low[f, row, :n, :], for_high[f, row, :n, :])
        even_ref[at : at + n, :] = jnp.where(odd_y, first, last)
        odd_ref[at : at + n, :] = jnp.where(odd_y, last, first)

    for at, d, f, n in corner_rows():
        put(at, f, H - d, n, True)
        put(at + CORNER // 2, f, d - 1, n, False)


def thirds(a):
    high = a.astype(jnp.bfloat16).astype(jnp.float32)
    rest = a - high
    middle = rest.astype(jnp.bfloat16).astype(jnp.float32)
    return high, middle, rest - middle


def products(load, pairs, groups, start=None):
    used = sorted({f for pair in pairs for f in pair})

    def body(g, totals):
        tile = {f: load(f, g) for f in used}
        return tuple(t + tile[i] * tile[j] for t, (i, j) in zip(totals, pairs))

    if start is None:
        start = (jnp.zeros((8, 128), jnp.float32),) * len(pairs)
    return lax.fori_loop(0, groups, body, start, unroll=16)


def early_kernel(prior_hbm, start_hbm, vel_hbm, out_ref, prior_ref, field, flow, sems):
    wx, wy = prior_ref.shape[1], prior_ref.shape[2]
    blocks = wy // 8
    parts = sems.shape[0] - 1
    part = wx // parts
    copies = []
    for k in range(parts):
        xs = pl.ds(k * part, part)
        inside = field.at[pl.ds(H + k * part, part), pl.ds(H, wy)]
        copies.append([
            pltpu.make_async_copy(prior_hbm.at[:, xs], prior_ref.at[:, xs], sems.at[k, 0]),
            pltpu.make_async_copy(start_hbm.at[xs], inside, sems.at[k, 1]),
        ])
        for c in copies[-1]:
            c.start()
    last = pltpu.make_async_copy(vel_hbm, flow.at[:, pl.ds(H, wx)], sems.at[parts, 0])
    last.start()

    totals = None
    for k in range(parts):
        for c in copies[k]:
            c.wait()

        def load(f, g, k=k):
            x, y = k * part + g // blocks, g % blocks * 8
            if f < 8:
                return prior_ref[f, x, pl.ds(pl.multiple_of(y, 8), 8), :]
            return field[H + x, pl.ds(pl.multiple_of(H + y, 8), 8), :]

        totals = products(load, EARLY, part * blocks, totals)
    for p, total in enumerate(totals):
        out_ref[p] = total
    last.wait()


def side(low, near, far):
    return pl.ds(pl.multiple_of(far - low * (far - near), H), H)


def coefficients(flow):
    lane = lax.broadcasted_iota(jnp.int32, (1, 1, 128), 2)
    a2 = DRIFT * flow[2]
    up = jnp.where(lane < 127, a2 - SIXTH, 0.0)
    down = jnp.where(lane > 0, -a2 - SIXTH, 0.0)
    return DRIFT * flow[0], DRIFT * flow[1], up, down


def stepped(src, x, n, y, size, keep, coefficient):
    here, ys = pl.ds(x, n), pl.ds(y, size)
    c = src[here, ys, :]
    e, w = src[pl.ds(x + 1, n), ys, :], src[pl.ds(x - 1, n), ys, :]
    u, d = src[here, pl.ds(y + 1, size), :], src[here, pl.ds(y - 1, size), :]
    a0, a1, up, down = coefficient
    above, below = pltpu.roll(c, 127, 2), pltpu.roll(c, 1, 2)
    return keep * c - SIXTH * ((e + w) + (u + d)) + a0 * (e - w) + a1 * (u - d) + (up * above + down * below)


def over_x(step, wx, rows, scale_low, scale_high, ready=None):
    def some(n):
        def body(i, carry):
            for k in range(0, n, 2):
                rows(H + (2 if ready else 0) + i * n + k, 2, None)
            return carry

        return body

    if ready:
        lax.fori_loop(0, 2, some(wx // 2 - 2), 0)
        ready()
        rows(H, 2, None)
        rows(H + wx - 2, 2, None)
    halo = STEPS - 1 - step
    for k in range(0, halo, 2):
        n = min(2, halo - k)
        rows(H - halo + k, n, scale_low)
        rows(H + wx + k, n, scale_high)
    if not ready:
        some(wx)(0, 0)


def late_products(fields, prior_ref, wx, blocks, acc, start):
    count = len(blocks)
    gap = blocks[1] - blocks[0]

    def load(f, g):
        x, y = g // count, blocks[0] * 8 + g % count * (gap * 8)
        if f < 8:
            return prior_ref[f, x, pl.ds(pl.multiple_of(y, 8), 8), :]
        return fields[f - 8][H + x, pl.ds(pl.multiple_of(H + y, 8), 8), :]

    n = len(EARLY)
    for pairs in (LATE, *CROSS):
        before = None
        if not start:
            before = tuple(acc[(n + p) * 8 : (n + p) * 8 + 8, :] for p in range(len(pairs)))
        for p, total in enumerate(products(load, pairs, wx * count, before)):
            acc[(n + p) * 8 : (n + p) * 8 + 8, :] = total
        n += len(pairs)


def inner_kernel(
    shifts_ref, place_ref, xe_ref, xo_ref, prior_ref, early_ref, field_in, flow_in, *rest
):
    fields, (flow, low, high, acc, coef, sems) = rest[:NEW], rest[NEW:]
    wx, wy = prior_ref.shape[1], prior_ref.shape[2]
    mid_y = pl.ds(H, wy)
    odd_x = place_ref[4]
    even_at, odd_at = side(odd_x, 0, H + wx), side(1 - odd_x, 0, H + wx)
    copies = [
        (xe_ref.at[0], fields[0].at[even_at, mid_y]),
        (xo_ref.at[0], fields[0].at[odd_at, mid_y]),
        (xe_ref.at[pl.ds(1, 3)], flow.at[:, even_at]),
        (xo_ref.at[pl.ds(1, 3)], flow.at[:, odd_at]),
    ]
    copies = [pltpu.make_async_copy(src, dst, sems.at[k]) for k, (src, dst) in enumerate(copies)]
    for c in copies:
        c.start()
    n = len(EARLY)
    acc[0 : n * 8, :] = early_ref[...].reshape(n * 8, 128)

    def ready():
        for c in copies:
            c.wait()

    x_low, x_high = (place_ref[k].astype(jnp.float32) for k in range(2))
    for step in range(STEPS):
        keep = 1.0 - shifts_ref[step]
        skip = 0 if step < 3 else 4 if step < 7 else 8

        def rows(x, n, scale, step=step, keep=keep, skip=skip):
            here, size = pl.ds(x, n), wy - 2 * skip
            if step == 0:
                cs = coefficients([flow[k, here, :, :] for k in range(3)])
                for k in range(4):
                    coef[k, here, :, :] = cs[k]
                    low[k, here, H:, :] = cs[k][:, :H]
                    high[k, here, :H, :] = cs[k][:, wy - H :]
            else:
                cs = [coef[k, here, pl.ds(skip, size), :] for k in range(4)]
            r = stepped(fields[step], x, n, H + skip, size, keep, cs)
            fields[step + 1][here, pl.ds(H + skip, size), :] = r if scale is None else r * scale

        over_x(step, wx, rows, x_low, x_high, ready if step == 0 else None)
    late_products(fields, prior_ref, wx, range(1, wy // 8 - 1), acc, True)


def outer_kernel(
    shifts_ref, place_ref, yo_ref, ye_ref, co_ref, ce_ref, prior_ref, acc_ref, *rest
):
    low, high, *fields = rest[NEW + 2 : 2 * NEW + 4]
    sums_ref, flow, acc, sems = rest[2 * NEW + 4 :]
    wx, wy = prior_ref.shape[1], prior_ref.shape[2]
    mid_x = pl.ds(H, wx)
    odd_y = place_ref[5]
    copies = []
    for ref, first in ((ye_ref, odd_y), (yo_ref, 1 - odd_y)):
        copies.append((ref.at[0], fields[0].at[mid_x, side(first, 0, H + wy)]))
        copies.append((ref.at[pl.ds(1, 3)], flow.at[:, mid_x, side(first, 0, H)]))
    copies = [pltpu.make_async_copy(src, dst, sems.at[k]) for k, (src, dst) in enumerate(copies)]
    for c in copies:
        c.start()
    acc[...] = acc_ref[...]
    for at, d, f, n in corner_rows():
        for x in (H - d, H + wx - 1 + d):
            even, odd = ce_ref[at : at + n, :], co_ref[at : at + n, :]
            ahead, behind = jnp.where(odd_y == 1, even, odd), jnp.where(odd_y == 1, odd, even)
            if f == 0:
                fields[0][x, H - n : H, :] = ahead
                fields[0][x, H + wy : H + wy + n, :] = behind
            else:
                flow[f - 1, x, H - n : H, :] = ahead
                flow[f - 1, x, H : H + n, :] = behind
            at += CORNER // 2
    for c in copies:
        c.wait()

    def prepare(i, carry):
        for m in range(0, 16, 2):
            here = pl.ds(i * 16 + m, 2)
            for out, ys in ((low, pl.ds(0, H)), (high, pl.ds(H, H))):
                for k, c in enumerate(coefficients([flow[k, here, ys, :] for k in range(3)])):
                    out[k, here, ys, :] = c
        return carry

    lax.fori_loop(0, (wx + 2 * H) // 16, prepare, 0)
    x_low, x_high, y_low, y_high = (place_ref[k].astype(jnp.float32) for k in range(4))
    row = lax.broadcasted_iota(jnp.int32, (1, 8, 128), 1)
    for step in range(STEPS):
        keep = 1.0 - shifts_ref[step]
        windows = (
            (H + step - 7, low, step + 1, jnp.where(row < 7 - step, y_low, 1.0)),
            (H + wy - 1 - step, high, 7 - step, jnp.where(row > step, y_high, 1.0)),
        )

        def rows(x, n, scale, step=step, keep=keep, windows=windows):
            here = pl.ds(x, n)
            for at, coef, first, inside in windows:
                cs = [coef[k, here, pl.ds(first, 8), :] for k in range(4)]
                r = stepped(fields[step], x, n, at, 8, keep, cs)
                if step < STEPS - 1:
                    r = r * (inside if scale is None else inside * scale)
                fields[step + 1][here, pl.ds(at, 8), :] = r

        over_x(step, wx, rows, x_low, x_high)
    late_products(fields, prior_ref, wx, (0, wy // 8 - 1), acc, False)
    n = len(PAIRS)
    acc[n * 8 :, :] = jnp.zeros((SLOTS * 8 - n * 8, 128), jnp.float32)
    by_lane = acc[pl.ds(0, SLOTS, stride=8), :]
    for s in range(1, 8):
        by_lane = by_lane + acc[pl.ds(s, SLOTS, stride=8), :]
    total = lax.dot_general(
        jnp.ones((8, 3 * 128), jnp.float32), jnp.concatenate(thirds(by_lane), axis=1), (((1,), (1,)), ((), ())),
        preferred_element_type=jnp.float32,
    )
    second = jnp.concatenate([total[:, 128:], jnp.zeros((8, 256 - SLOTS), jnp.float32)], axis=1)
    even = lax.broadcasted_iota(jnp.int32, (8, 128), 0) % 2 == 0
    both = jnp.where(even, total[:, :128], second)
    sums_ref[...] = both


def combine_kernel(
    count, chunks, sums_ref, first_ref, second_ref, prior_ref, *rest
):
    fields, (new_hbm, coeffs_ref, new, spread, out_sems) = rest[:NEW], rest[NEW:]
    wx, wy = prior_ref.shape[1], prior_ref.shape[2]
    part = wx // chunks
    total = sums_ref[0:8, :]
    for k in range(1, sums_ref.shape[0] // 8):
        total = total + sums_ref[k * 8 : k * 8 + 8, :]
    total = total + pltpu.roll(total, 4, 0)
    total = (total + pltpu.roll(total, 2, 0)) * (1.0 / count)
    flat = jnp.concatenate([total[0:1, :], total[1:2, :]], axis=1)
    first, second = first_ref[:24], second_ref[:24]

    def contract(left, right):
        rows = jnp.concatenate([left * part_of for part_of in thirds(flat)], axis=0)
        r = lax.dot_general(rows, right[...], (((1,), (1,)), ((), ())), preferred_element_type=jnp.float32)
        return (r[:24] + r[24:48]) + r[48:]

    full = contract(first, second_ref) + contract(second, first_ref)
    top, low = full[0:8, :], full[8:24, :]
    inner = 2.0 * top
    for k in range(PRIOR):
        inner = inner - top[:, k : k + 1] * top[k : k + 1, :]
    gram = low
    for k in range(PRIOR):
        gram = gram - low[:, k : k + 1] * inner[k : k + 1, :]
    lane = lax.broadcasted_iota(jnp.int32, (16, 128), 1)
    row = lax.broadcasted_iota(jnp.int32, (16, 128), 0)
    columns = [jnp.broadcast_to(gram[:, PRIOR + k : PRIOR + k + 1], (16, 128)) for k in range(NEW)]
    units = [jnp.where(row == k, 1.0, 0.0) for k in range(NEW)]
    coefs = [jnp.broadcast_to(low[:, k : k + 1], (16, 128)) for k in range(PRIOR)]
    pivots = jnp.ones((16, 128), jnp.float32)
    for k in range(NEW):
        pivot = columns[k][k : k + 1, :]
        pivots = jnp.where(row == k, pivot, pivots)
        factor = jnp.where(row > k, columns[k] * (1.0 / pivot), 0.0)
        columns[k + 1 :] = [c - factor * c[k : k + 1, :] for c in columns[k + 1 :]]
        units[: k + 1] = [c - factor * c[k : k + 1, :] for c in units[: k + 1]]
        coefs = [c - factor * c[k : k + 1, :] for c in coefs]
    scale = 1.0 / jnp.sqrt(pivots)
    for i, c in enumerate(units + coefs):
        spread[i] = c * scale
    upper = jnp.zeros((16, 128), jnp.float32)
    for k in range(NEW):
        upper = jnp.where((lane == k) & (row <= k), columns[k] * scale, upper)
    both = jnp.concatenate([pltpu.roll(top, 128 - PRIOR, 1), upper], axis=0)
    stores = []
    for k in range(chunks):
        def some(g, carry, k=k):
            x, y = k * part + g // (wy // 16), g % (wy // 16)
            ys = pl.ds(pl.multiple_of(y * 16, 16), 16)
            inner = pl.ds(pl.multiple_of(H + y * 16, 8), 16)
            tiles = [fields[i][H + x, inner, :] for i in range(NEW)]
            tiles += [prior_ref[i, x, ys, :] for i in range(PRIOR)]
            for j in range(NEW):
                r = spread[0, j : j + 1, :] * tiles[0]
                for i in range(1, j + 1):
                    r = r + spread[i, j : j + 1, :] * tiles[i]
                for i in range(NEW, FIELDS):
                    r = r - spread[i, j : j + 1, :] * tiles[i]
                new[j, x, ys, :] = r
            return carry

        lax.fori_loop(0, part * (wy // 16), some, 0, unroll=2)
        xs = pl.ds(k * part, part)
        stores.append(pltpu.make_async_copy(new.at[:, xs], new_hbm.at[:, xs], out_sems.at[k]))
        stores[-1].start()
    both = jnp.concatenate([both, jnp.zeros((104, 128), jnp.float32)], axis=0)
    coeffs_ref[...] = both.T[:NEW, :FIELDS]
    for c in stores:
        c.wait()


def on_device(start, velocity, prior, shifts):
    wx, wy, wz = start.shape
    nx, ny = lax.axis_size("gx"), lax.axis_size("gy")
    devices = nx * ny
    swaps = {
        axis: [[pair for i in range(odd, n - 1, 2) for pair in ((i, i + 1), (i + 1, i))] for odd in (0, 1)]
        for axis, n in (("gx", nx), ("gy", ny))
    }
    ix, iy = lax.axis_index("gx"), lax.axis_index("gy")
    place = jnp.stack([ix > 0, ix < nx - 1, iy > 0, iy < ny - 1, ix % 2 == 1, iy % 2 == 1]).astype(jnp.int32)

    f32 = jnp.float32
    vmem = pl.BlockSpec(memory_space=pltpu.VMEM)
    smem = pl.BlockSpec(memory_space=pltpu.SMEM)
    hbm = pl.BlockSpec(memory_space=pl.ANY)
    limit = pltpu.CompilerParams(vmem_limit_bytes=12 * 1024 * 1024)
    edge_y = jax.ShapeDtypeStruct((4, wx, H, wz), f32)
    edge_x = jax.ShapeDtypeStruct((4, H, wy, wz), f32)
    corner = jax.ShapeDtypeStruct((CORNER, wz), f32)
    start_hbm, velocity_hbm, prior_hbm = (
        pltpu.with_memory_space_constraint(v, pltpu.HBM) for v in (start, velocity, prior)
    )
    y_even, y_odd, x_even, x_odd = pl.pallas_call(
        pack_kernel,
        out_shape=(edge_y, edge_y, edge_x, edge_x),
        in_specs=[smem, hbm, hbm],
        out_specs=(vmem,) * 4,
        scratch_shapes=[pltpu.SemaphoreType.DMA((8,))],
        compiler_params=limit,
        name="pack",
    )(place, start_hbm, velocity_hbm)
    xo = lax.ppermute(x_odd, "gx", swaps["gx"][1])
    xe = lax.ppermute(x_even, "gx", swaps["gx"][0])
    yo = lax.ppermute(y_odd, "gy", swaps["gy"][1])
    ye = lax.ppermute(y_even, "gy", swaps["gy"][0])
    ex, ey = wx + 2 * H, wy + 2 * H
    field = pltpu.VMEM((ex, ey, wz), f32)
    flow = pltpu.VMEM((3, ex, wy, wz), f32)
    strip = pltpu.VMEM((4, ex, 2 * H, wz), f32)
    early, prior_in, first, flows = pl.pallas_call(
        early_kernel,
        out_shape=(
            jax.ShapeDtypeStruct((len(EARLY), 8, 128), f32),
            pltpu.VMEM(prior.shape, f32),
            field,
            flow,
        ),
        in_specs=[hbm] * 3,
        out_specs=(vmem,) * 4,
        scratch_shapes=[pltpu.SemaphoreType.DMA((9, 2))],
        compiler_params=limit,
        name="early",
    )(prior_hbm, start_hbm, velocity_hbm)
    xe, xo, early = lax.optimization_barrier((xe, xo, early))
    c_even, c_odd = pl.pallas_call(
        corner_kernel,
        out_shape=(corner, corner),
        in_specs=[smem, vmem, vmem],
        out_specs=(vmem, vmem),
        compiler_params=limit,
        name="corner",
    )(place, xe, xo)
    co = lax.ppermute(c_odd, "gy", swaps["gy"][1])
    ce = lax.ppermute(c_even, "gy", swaps["gy"][0])
    *fields, flows, low, high, acc = pl.pallas_call(
        inner_kernel,
        out_shape=(*[field] * NEW, flow, strip, strip, pltpu.VMEM((SLOTS * 8, 128), f32)),
        in_specs=[smem, smem, hbm, hbm] + [vmem] * 4,
        out_specs=(vmem,) * (NEW + 4),
        scratch_shapes=[pltpu.VMEM((4, ex, wy, wz), f32), pltpu.SemaphoreType.DMA((4,))],
        input_output_aliases={6: 0, 7: NEW},
        compiler_params=limit,
        name="inner",
    )(shifts, place, xe, xo, prior_in, early, first, flows)
    low, high, *fields, sums = pl.pallas_call(
        outer_kernel,
        out_shape=(strip, strip, *[field] * NEW, jax.ShapeDtypeStruct((8, 128), f32)),
        in_specs=[smem, smem, hbm, hbm] + [vmem] * (6 + NEW),
        out_specs=(vmem,) * (NEW + 3),
        scratch_shapes=[
            pltpu.VMEM((3, ex, 2 * H, wz), f32),
            pltpu.VMEM((SLOTS * 8, 128), f32),
            pltpu.SemaphoreType.DMA((4,)),
        ],
        input_output_aliases={8 + k: k for k in range(NEW + 2)},
        compiler_params=limit,
        name="outer",
    )(shifts, place, yo, ye, co, ce, prior_in, acc, low, high, *fields)
    sums = sums + lax.ppermute(sums, "gx", swaps["gx"][0])
    chips = devices // 2
    cores = [[x * ny + y for x in range(core, nx, 2) for y in range(ny)] for core in (0, 1)]
    sums = jnp.broadcast_to(sums[None], (chips // 4, 8, 128)).reshape(chips * 2, 128)
    every = lax.all_to_all(sums, AXES, 0, 0, tiled=True, axis_index_groups=cores)
    chunks = 8
    first, second = pair_tables()
    basis_new, coeffs = pl.pallas_call(
        functools.partial(combine_kernel, float(devices * wx * wy * wz), chunks),
        out_shape=(
            jax.ShapeDtypeStruct((NEW, wx, wy, wz), f32),
            jax.ShapeDtypeStruct((NEW, FIELDS), f32),
        ),
        in_specs=[vmem] * (4 + NEW),
        out_specs=(hbm, vmem),
        scratch_shapes=[
            pltpu.VMEM((NEW, wx, wy, wz), f32),
            pltpu.VMEM((FIELDS, 16, 128), f32),
            pltpu.SemaphoreType.DMA((chunks,)),
        ],
        compiler_params=limit,
        name="combine",
    )(every, jnp.asarray(first), jnp.asarray(second), prior_in, *fields)
    return basis_new, coeffs.T


def solution(mesh):
    return jax.shard_map(
        on_device,
        mesh=mesh,
        in_specs=(P("gx", "gy", None), P(None, "gx", "gy", None), P(None, "gx", "gy", None), P()),
        out_specs=(P(None, "gx", "gy", None), P()),
        check_vma=False,
    )
```

```python
import functools

import jax
import jax.numpy as jnp
import numpy as np
from jax import lax
from jax.experimental import pallas as pl
from jax.experimental.pallas import tpu as pltpu
from jax.sharding import PartitionSpec as P

STEPS = 8
PRIOR = 8
NEW = STEPS + 1
FIELDS = PRIOR + NEW
H = STEPS
DRIFT = 0.3
SIXTH = 1.0 / 6.0
AXES = ("gx", "gy")

EARLY = [(i, j) for i in range(9) for j in range(i, 9)]
LATE = [(i, j) for i in range(9, 17) for j in range(i, 17)]
CROSS = [[(i, j) for i in range(9) for j in range(lo, lo + 4)] for lo in (9, 13)]
PAIRS = EARLY + LATE + CROSS[0] + CROSS[1]
SLOTS = 160


def pair_tables():
    first = np.zeros((128, 256), np.float32)
    second = np.zeros((128, 256), np.float32)
    for p, (i, j) in enumerate(PAIRS):
        first[i, p] = 0.5 if i == j else 1.0
        second[j, p] = 1.0
    return first, second


def corner_rows():
    at, pieces = 0, []
    for d in range(1, H):
        for f in range(4):
            n = H - d if f == 0 else H - 1 - d
            if n:
                pieces.append((at, d, f, n))
            at += n
    return pieces


CORNER = 2 * sum(n for _, _, _, n in corner_rows())


def pack_kernel(place_ref, start_ref, vel_ref, y_even, y_odd, x_even, x_odd, sems):
    wx, wy = start_ref.shape[0], start_ref.shape[1]
    full = slice(None)
    odd_x, odd_y = place_ref[4], place_ref[5]

    def cut(n, odd):
        return pl.ds(pl.multiple_of((n - H) * odd, H), H)

    copies = []
    for out, where in (
        (x_odd, (cut(wx, odd_x), full)),
        (x_even, (cut(wx, 1 - odd_x), full)),
        (y_odd, (full, cut(wy, odd_y))),
        (y_even, (full, cut(wy, 1 - odd_y))),
    ):
        copies.append((start_ref.at[where], out.at[0]))
        copies.append((vel_ref.at[(full, *where)], out.at[pl.ds(1, 3)]))
    copies = [pltpu.make_async_copy(src, dst, sems.at[k]) for k, (src, dst) in enumerate(copies)]
    for c in copies:
        c.start()
    for c in copies:
        c.wait()


def corner_kernel(place_ref, xe_ref, xo_ref, even_ref, odd_ref):
    wy = xe_ref.shape[2]
    odd_x, odd_y = place_ref[4] == 1, place_ref[5] == 1

    def put(at, f, row, n, low):
        for_low, for_high = (xe_ref, xo_ref) if low else (xo_ref, xe_ref)
        last = jnp.where(odd_x, for_low[f, row, wy - 8 :, :], for_high[f, row, wy - 8 :, :])[8 - n :]
        first = jnp.where(odd_x, for_low[f, row, :8, :], for_high[f, row, :8, :])[:n]
        even_ref[at : at + n, :] = jnp.where(odd_y, first, last)
        odd_ref[at : at + n, :] = jnp.where(odd_y, last, first)

    for at, d, f, n in corner_rows():
        put(at, f, H - d, n, True)
        put(at + CORNER // 2, f, d - 1, n, False)


def thirds(a):
    high = a.astype(jnp.bfloat16).astype(jnp.float32)
    rest = a - high
    middle = rest.astype(jnp.bfloat16).astype(jnp.float32)
    return high, middle, rest - middle


def products(load, pairs, groups, start=None):
    used = sorted({f for pair in pairs for f in pair})

    def body(g, totals):
        tile = {f: load(f, g) for f in used}
        return tuple(t + tile[i] * tile[j] for t, (i, j) in zip(totals, pairs))

    if start is None:
        start = (jnp.zeros((8, 128), jnp.float32),) * len(pairs)
    return lax.fori_loop(0, groups, body, start, unroll=16)


def early_kernel(prior_hbm, start_hbm, vel_hbm, out_ref, prior_ref, field, flow, sems):
    wx, wy = prior_ref.shape[1], prior_ref.shape[2]
    blocks = wy // 8
    parts = sems.shape[0] - 1
    part = wx // parts
    copies = []
    for k in range(parts):
        xs = pl.ds(k * part, part)
        inside = field.at[pl.ds(H + k * part, part), pl.ds(H, wy)]
        copies.append([
            pltpu.make_async_copy(prior_hbm.at[:, xs], prior_ref.at[:, xs], sems.at[k, 0]),
            pltpu.make_async_copy(start_hbm.at[xs], inside, sems.at[k, 1]),
        ])
        for c in copies[-1]:
            c.start()
    last = pltpu.make_async_copy(vel_hbm, flow.at[:, pl.ds(H, wx)], sems.at[parts, 0])
    last.start()

    totals = None
    for k in range(parts):
        for c in copies[k]:
            c.wait()

        def load(f, g, k=k):
            x, y = k * part + g // blocks, g % blocks * 8
            if f < 8:
                return prior_ref[f, x, pl.ds(pl.multiple_of(y, 8), 8), :]
            return field[H + x, pl.ds(pl.multiple_of(H + y, 8), 8), :]

        totals = products(load, EARLY, part * blocks, totals)
    for p, total in enumerate(totals):
        out_ref[p] = total
    last.wait()


def side(low, near, far):
    return pl.ds(pl.multiple_of(far - low * (far - near), H), H)


def coefficients(flow):
    lane = lax.broadcasted_iota(jnp.int32, (1, 1, 128), 2)
    a2 = DRIFT * flow[2]
    up = jnp.where(lane < 127, a2 - SIXTH, 0.0)
    down = jnp.where(lane > 0, -a2 - SIXTH, 0.0)
    return DRIFT * flow[0], DRIFT * flow[1], up, down


def stepped(src, x, n, y, size, keep, coefficient):
    here, ys = pl.ds(x, n), pl.ds(y, size)
    c = src[here, ys, :]
    e, w = src[pl.ds(x + 1, n), ys, :], src[pl.ds(x - 1, n), ys, :]
    u, d = src[here, pl.ds(y + 1, size), :], src[here, pl.ds(y - 1, size), :]
    a0, a1, up, down = coefficient
    above, below = pltpu.roll(c, 127, 2), pltpu.roll(c, 1, 2)
    return keep * c - SIXTH * ((e + w) + (u + d)) + a0 * (e - w) + a1 * (u - d) + (up * above + down * below)


def over_x(step, wx, rows, scale_low, scale_high, ready=None):
    def some(n):
        def body(i, carry):
            for k in range(0, n, 2):
                rows(H + (2 if ready else 0) + i * n + k, 2, None)
            return carry

        return body

    if ready:
        lax.fori_loop(0, 2, some(wx // 2 - 2), 0)
        ready()
        rows(H, 2, None)
        rows(H + wx - 2, 2, None)
    halo = STEPS - 1 - step
    for k in range(0, halo, 2):
        n = min(2, halo - k)
        rows(H - halo + k, n, scale_low)
        rows(H + wx + k, n, scale_high)
    if not ready:
        some(wx)(0, 0)


def late_products(fields, prior_ref, wx, blocks, acc, start):
    count = len(blocks)
    gap = blocks[1] - blocks[0]

    def load(f, g):
        x, y = g // count, blocks[0] * 8 + g % count * (gap * 8)
        if f < 8:
            return prior_ref[f, x, pl.ds(pl.multiple_of(y, 8), 8), :]
        return fields[f - 8][H + x, pl.ds(pl.multiple_of(H + y, 8), 8), :]

    n = len(EARLY)
    for pairs in (LATE, *CROSS):
        before = None
        if not start:
            before = tuple(acc[(n + p) * 8 : (n + p) * 8 + 8, :] for p in range(len(pairs)))
        for p, total in enumerate(products(load, pairs, wx * count, before)):
            acc[(n + p) * 8 : (n + p) * 8 + 8, :] = total
        n += len(pairs)


def inner_kernel(
    shifts_ref, place_ref, xe_ref, xo_ref, prior_ref, early_ref, field_in, flow_in, *rest
):
    fields, (flow, low, high, acc, coef, sems) = rest[:NEW], rest[NEW:]
    wx, wy = prior_ref.shape[1], prior_ref.shape[2]
    mid_y = pl.ds(H, wy)
    odd_x = place_ref[4]
    even_at, odd_at = side(odd_x, 0, H + wx), side(1 - odd_x, 0, H + wx)
    copies = [
        (xe_ref.at[0], fields[0].at[even_at, mid_y]),
        (xo_ref.at[0], fields[0].at[odd_at, mid_y]),
        (xe_ref.at[pl.ds(1, 3)], flow.at[:, even_at]),
        (xo_ref.at[pl.ds(1, 3)], flow.at[:, odd_at]),
    ]
    copies = [pltpu.make_async_copy(src, dst, sems.at[k]) for k, (src, dst) in enumerate(copies)]
    for c in copies:
        c.start()
    n = len(EARLY)
    acc[0 : n * 8, :] = early_ref[...].reshape(n * 8, 128)

    def ready():
        for c in copies:
            c.wait()

    x_low, x_high = (place_ref[k].astype(jnp.float32) for k in range(2))
    for step in range(STEPS):
        keep = 1.0 - shifts_ref[step]
        skip = 0 if step < 3 else 4 if step < 7 else 8

        def rows(x, n, scale, step=step, keep=keep, skip=skip):
            here, size = pl.ds(x, n), wy - 2 * skip
            if step == 0:
                cs = coefficients([flow[k, here, :, :] for k in range(3)])
                for k in range(4):
                    coef[k, here, :, :] = cs[k]
                    low[k, here, H:, :] = cs[k][:, :H]
                    high[k, here, :H, :] = cs[k][:, wy - H :]
            else:
                cs = [coef[k, here, pl.ds(skip, size), :] for k in range(4)]
            r = stepped(fields[step], x, n, H + skip, size, keep, cs)
            fields[step + 1][here, pl.ds(H + skip, size), :] = r if scale is None else r * scale

        over_x(step, wx, rows, x_low, x_high, ready if step == 0 else None)
    late_products(fields, prior_ref, wx, range(1, wy // 8 - 1), acc, True)


def outer_kernel(
    shifts_ref, place_ref, yo_ref, ye_ref, co_ref, ce_ref, prior_ref, acc_ref, *rest
):
    low, high, *fields = rest[NEW + 2 : 2 * NEW + 4]
    sums_ref, flow, acc, sems = rest[2 * NEW + 4 :]
    wx, wy = prior_ref.shape[1], prior_ref.shape[2]
    mid_x = pl.ds(H, wx)
    odd_y = place_ref[5]
    copies = []
    for ref, first in ((ye_ref, odd_y), (yo_ref, 1 - odd_y)):
        copies.append((ref.at[0], fields[0].at[mid_x, side(first, 0, H + wy)]))
        copies.append((ref.at[pl.ds(1, 3)], flow.at[:, mid_x, side(first, 0, H)]))
    copies = [pltpu.make_async_copy(src, dst, sems.at[k]) for k, (src, dst) in enumerate(copies)]
    for c in copies:
        c.start()
    acc[...] = acc_ref[...]
    for at, d, f, n in corner_rows():
        for x in (H - d, H + wx - 1 + d):
            even, odd = ce_ref[at : at + n, :], co_ref[at : at + n, :]
            ahead, behind = jnp.where(odd_y == 1, even, odd), jnp.where(odd_y == 1, odd, even)
            if f == 0:
                fields[0][x, H - n : H, :] = ahead
                fields[0][x, H + wy : H + wy + n, :] = behind
            else:
                flow[f - 1, x, H - n : H, :] = ahead
                flow[f - 1, x, H : H + n, :] = behind
            at += CORNER // 2
    for c in copies:
        c.wait()

    def prepare(i, carry):
        for m in range(0, 16, 2):
            here = pl.ds(i * 16 + m, 2)
            for out, ys in ((low, pl.ds(0, H)), (high, pl.ds(H, H))):
                for k, c in enumerate(coefficients([flow[k, here, ys, :] for k in range(3)])):
                    out[k, here, ys, :] = c
        return carry

    lax.fori_loop(0, (wx + 2 * H) // 16, prepare, 0)
    x_low, x_high, y_low, y_high = (place_ref[k].astype(jnp.float32) for k in range(4))
    row = lax.broadcasted_iota(jnp.int32, (1, 8, 128), 1)
    for step in range(STEPS):
        keep = 1.0 - shifts_ref[step]
        windows = (
            (H + step - 7, low, step + 1, jnp.where(row < 7 - step, y_low, 1.0)),
            (H + wy - 1 - step, high, 7 - step, jnp.where(row > step, y_high, 1.0)),
        )

        def rows(x, n, scale, step=step, keep=keep, windows=windows):
            here = pl.ds(x, n)
            for at, coef, first, inside in windows:
                cs = [coef[k, here, pl.ds(first, 8), :] for k in range(4)]
                r = stepped(fields[step], x, n, at, 8, keep, cs)
                if step < STEPS - 1:
                    r = r * (inside if scale is None else inside * scale)
                fields[step + 1][here, pl.ds(at, 8), :] = r

        over_x(step, wx, rows, x_low, x_high)
    late_products(fields, prior_ref, wx, (0, wy // 8 - 1), acc, False)
    n = len(PAIRS)
    acc[n * 8 :, :] = jnp.zeros((SLOTS * 8 - n * 8, 128), jnp.float32)
    by_lane = acc[pl.ds(0, SLOTS, stride=8), :]
    for s in range(1, 8):
        by_lane = by_lane + acc[pl.ds(s, SLOTS, stride=8), :]
    total = lax.dot_general(
        jnp.ones((8, 3 * 128), jnp.float32), jnp.concatenate(thirds(by_lane), axis=1), (((1,), (1,)), ((), ())),
        preferred_element_type=jnp.float32,
    )
    second = jnp.concatenate([total[:, 128:], jnp.zeros((8, 256 - SLOTS), jnp.float32)], axis=1)
    even = lax.broadcasted_iota(jnp.int32, (8, 128), 0) % 2 == 0
    both = jnp.where(even, total[:, :128], second)
    sums_ref[...] = both


def combine_kernel(
    count, chunks, sums_ref, first_ref, second_ref, prior_ref, *rest
):
    fields, (new_hbm, coeffs_ref, new, spread, out_sems) = rest[:NEW], rest[NEW:]
    wx, wy = prior_ref.shape[1], prior_ref.shape[2]
    part = wx // chunks
    total = sums_ref[0:8, :]
    for k in range(1, sums_ref.shape[0] // 8):
        total = total + sums_ref[k * 8 : k * 8 + 8, :]
    total = total + pltpu.roll(total, 4, 0)
    total = (total + pltpu.roll(total, 2, 0)) * (1.0 / count)
    flat = jnp.concatenate([total[0:1, :], total[1:2, :]], axis=1)
    first, second = first_ref[:24], second_ref[:24]

    def contract(left, right):
        rows = jnp.concatenate([left * part_of for part_of in thirds(flat)], axis=0)
        r = lax.dot_general(rows, right[...], (((1,), (1,)), ((), ())), preferred_element_type=jnp.float32)
        return (r[:24] + r[24:48]) + r[48:]

    full = contract(first, second_ref) + contract(second, first_ref)
    top, low = full[0:8, :], full[8:24, :]
    inner = 2.0 * top
    for k in range(PRIOR):
        inner = inner - top[:, k : k + 1] * top[k : k + 1, :]
    gram = low
    for k in range(PRIOR):
        gram = gram - low[:, k : k + 1] * inner[k : k + 1, :]
    lane = lax.broadcasted_iota(jnp.int32, (16, 128), 1)
    row = lax.broadcasted_iota(jnp.int32, (16, 128), 0)
    columns = [jnp.broadcast_to(gram[:, PRIOR + k : PRIOR + k + 1], (16, 128)) for k in range(NEW)]
    units = [jnp.where(row == k, 1.0, 0.0) for k in range(NEW)]
    coefs = [jnp.broadcast_to(low[:, k : k + 1], (16, 128)) for k in range(PRIOR)]
    pivots = jnp.ones((16, 128), jnp.float32)
    for k in range(NEW):
        pivot = columns[k][k : k + 1, :]
        pivots = jnp.where(row == k, pivot, pivots)
        factor = jnp.where(row > k, columns[k] * (1.0 / pivot), 0.0)
        columns[k + 1 :] = [c - factor * c[k : k + 1, :] for c in columns[k + 1 :]]
        units[: k + 1] = [c - factor * c[k : k + 1, :] for c in units[: k + 1]]
        coefs = [c - factor * c[k : k + 1, :] for c in coefs]
    scale = 1.0 / jnp.sqrt(pivots)
    for i, c in enumerate(units + coefs):
        spread[i] = c * scale
    upper = jnp.zeros((16, 128), jnp.float32)
    for k in range(NEW):
        upper = jnp.where((lane == k) & (row <= k), columns[k] * scale, upper)
    both = jnp.concatenate([pltpu.roll(top, 128 - PRIOR, 1), upper], axis=0)
    stores = []
    for k in range(chunks):
        def some(g, carry, k=k):
            x, y = k * part + g // (wy // 16), g % (wy // 16)
            ys = pl.ds(pl.multiple_of(y * 16, 16), 16)
            inner = pl.ds(pl.multiple_of(H + y * 16, 8), 16)
            tiles = [fields[i][H + x, inner, :] for i in range(NEW)]
            tiles += [prior_ref[i, x, ys, :] for i in range(PRIOR)]
            for j in range(NEW):
                r = spread[0, j : j + 1, :] * tiles[0]
                for i in range(1, j + 1):
                    r = r + spread[i, j : j + 1, :] * tiles[i]
                for i in range(NEW, FIELDS):
                    r = r - spread[i, j : j + 1, :] * tiles[i]
                new[j, x, ys, :] = r
            return carry

        lax.fori_loop(0, part * (wy // 16), some, 0, unroll=2)
        xs = pl.ds(k * part, part)
        stores.append(pltpu.make_async_copy(new.at[:, xs], new_hbm.at[:, xs], out_sems.at[k]))
        stores[-1].start()
    both = jnp.concatenate([both, jnp.zeros((104, 128), jnp.float32)], axis=0)
    coeffs_ref[...] = both.T[:NEW, :FIELDS]
    for c in stores:
        c.wait()


def on_device(start, velocity, prior, shifts):
    wx, wy, wz = start.shape
    nx, ny = lax.axis_size("gx"), lax.axis_size("gy")
    devices = nx * ny
    swaps = {
        axis: [[pair for i in range(odd, n - 1, 2) for pair in ((i, i + 1), (i + 1, i))] for odd in (0, 1)]
        for axis, n in (("gx", nx), ("gy", ny))
    }
    ix, iy = lax.axis_index("gx"), lax.axis_index("gy")
    place = jnp.stack([ix > 0, ix < nx - 1, iy > 0, iy < ny - 1, ix % 2 == 1, iy % 2 == 1]).astype(jnp.int32)

    f32 = jnp.float32
    vmem = pl.BlockSpec(memory_space=pltpu.VMEM)
    smem = pl.BlockSpec(memory_space=pltpu.SMEM)
    hbm = pl.BlockSpec(memory_space=pl.ANY)
    limit = pltpu.CompilerParams(vmem_limit_bytes=12 * 1024 * 1024)
    edge_y = jax.ShapeDtypeStruct((4, wx, H, wz), f32)
    edge_x = jax.ShapeDtypeStruct((4, H, wy, wz), f32)
    corner = jax.ShapeDtypeStruct((CORNER + 10, wz), f32)
    start_hbm, velocity_hbm, prior_hbm = (
        pltpu.with_memory_space_constraint(v, pltpu.HBM) for v in (start, velocity, prior)
    )
    y_even, y_odd, x_even, x_odd = pl.pallas_call(
        pack_kernel,
        out_shape=(edge_y, edge_y, edge_x, edge_x),
        in_specs=[smem, hbm, hbm],
        out_specs=(vmem,) * 4,
        scratch_shapes=[pltpu.SemaphoreType.DMA((8,))],
        compiler_params=limit,
        name="pack",
    )(place, start_hbm, velocity_hbm)
    xo = lax.ppermute(x_odd, "gx", swaps["gx"][1])
    xe = lax.ppermute(x_even, "gx", swaps["gx"][0])
    yo = lax.ppermute(y_odd, "gy", swaps["gy"][1])
    ye = lax.ppermute(y_even, "gy", swaps["gy"][0])
    ex, ey = wx + 2 * H, wy + 2 * H
    field = pltpu.VMEM((ex, ey, wz), f32)
    flow = pltpu.VMEM((3, ex, wy, wz), f32)
    strip = pltpu.VMEM((4, ex, 2 * H, wz), f32)
    early, prior_in, first, flows = pl.pallas_call(
        early_kernel,
        out_shape=(
            jax.ShapeDtypeStruct((len(EARLY), 8, 128), f32),
            pltpu.VMEM(prior.shape, f32),
            field,
            flow,
        ),
        in_specs=[hbm] * 3,
        out_specs=(vmem,) * 4,
        scratch_shapes=[pltpu.SemaphoreType.DMA((9, 2))],
        compiler_params=limit,
        name="early",
    )(prior_hbm, start_hbm, velocity_hbm)
    xe, xo, early = lax.optimization_barrier((xe, xo, early))
    c_even, c_odd = pl.pallas_call(
        corner_kernel,
        out_shape=(corner, corner),
        in_specs=[smem, vmem, vmem],
        out_specs=(vmem, vmem),
        compiler_params=limit,
        name="corner",
    )(place, xe, xo)
    co = lax.ppermute(c_odd, "gy", swaps["gy"][1])
    ce = lax.ppermute(c_even, "gy", swaps["gy"][0])
    *fields, flows, low, high, acc = pl.pallas_call(
        inner_kernel,
        out_shape=(*[field] * NEW, flow, strip, strip, pltpu.VMEM((SLOTS * 8, 128), f32)),
        in_specs=[smem, smem, hbm, hbm] + [vmem] * 4,
        out_specs=(vmem,) * (NEW + 4),
        scratch_shapes=[pltpu.VMEM((4, ex, wy, wz), f32), pltpu.SemaphoreType.DMA((4,))],
        input_output_aliases={6: 0, 7: NEW},
        compiler_params=limit,
        name="inner",
    )(shifts, place, xe, xo, prior_in, early, first, flows)
    low, high, *fields, sums = pl.pallas_call(
        outer_kernel,
        out_shape=(strip, strip, *[field] * NEW, jax.ShapeDtypeStruct((8, 128), f32)),
        in_specs=[smem, smem, hbm, hbm] + [vmem] * (6 + NEW),
        out_specs=(vmem,) * (NEW + 3),
        scratch_shapes=[
            pltpu.VMEM((3, ex, 2 * H, wz), f32),
            pltpu.VMEM((SLOTS * 8, 128), f32),
            pltpu.SemaphoreType.DMA((4,)),
        ],
        input_output_aliases={8 + k: k for k in range(NEW + 2)},
        compiler_params=limit,
        name="outer",
    )(shifts, place, yo, ye, co, ce, prior_in, acc, low, high, *fields)
    sums = sums + lax.ppermute(sums, "gx", swaps["gx"][0])
    chips = devices // 2
    cores = [[x * ny + y for x in range(core, nx, 2) for y in range(ny)] for core in (0, 1)]
    sums = jnp.broadcast_to(sums[None], (chips // 4, 8, 128)).reshape(chips * 2, 128)
    every = lax.all_to_all(sums, AXES, 0, 0, tiled=True, axis_index_groups=cores)
    chunks = 8
    first, second = pair_tables()
    basis_new, coeffs = pl.pallas_call(
        functools.partial(combine_kernel, float(devices * wx * wy * wz), chunks),
        out_shape=(
            jax.ShapeDtypeStruct((NEW, wx, wy, wz), f32),
            jax.ShapeDtypeStruct((NEW, FIELDS), f32),
        ),
        in_specs=[vmem] * (4 + NEW),
        out_specs=(hbm, vmem),
        scratch_shapes=[
            pltpu.VMEM((NEW, wx, wy, wz), f32),
            pltpu.VMEM((FIELDS, 16, 128), f32),
            pltpu.SemaphoreType.DMA((chunks,)),
        ],
        compiler_params=limit,
        name="combine",
    )(every, jnp.asarray(first), jnp.asarray(second), prior_in, *fields)
    return basis_new, coeffs.T


def solution(mesh):
    return jax.shard_map(
        on_device,
        mesh=mesh,
        in_specs=(P("gx", "gy", None), P(None, "gx", "gy", None), P(None, "gx", "gy", None), P()),
        out_specs=(P(None, "gx", "gy", None), P()),
        check_vma=False,
    )
```
